256 devices in a mesh: depth: 32 (over y, z), rows: 8 (over x, core).
Axes of the slice: x: 4, y: 4, z: 8, core: 2. Of those that a mesh axis runs over, the one named last changes fastest.
Arguments:
- field: bfloat16 [512, 512, 1024], P('depth', 'rows'), may hold values from -6 to 6
- tf_centers: float32 [4], replicated, may hold values from -1.5 to 1.5
- tf_widths: float32 [4], replicated, may hold values from 0.4 to 1.2
- tf_density: float32 [4], replicated, may hold values from 0.5 to 4
- tf_colors: float32 [3, 4], replicated, may hold values from 0.1 to 1
- light: float32 [3], replicated, may hold values from 0.5 to 1.5
Outputs:
- image: float32 [4, 512, 1024], P(None, 'rows', 'depth')
The draws below stay inside these ranges and needn't reach their ends.
All inputs are finite; a program needn't handle non-finite values.
Results may differ from the reference program's by a relative error of at most 0.0003.
Values may be sent and summed in bfloat16 or wider, within the bound.
No kernel may reach another device: no remote copies, remote signals or barrier semaphores. Data moves between devices by JAX's collectives and lax.ppermute only.
A program may use at most 64 MiB of HBM per device.

```python
import math
import jax
import jax.numpy as jnp
from jax import lax

YD = 64
NX = 1024
BUMPS = 4
NZ = 512
NY = 512


def steps_of(rng, shape, cuts, smallest, largest):
    def one(dim, shards_of):
        heights = jax.random.uniform(jax.random.fold_in(jax.random.fold_in(rng, 6), dim), (shards_of,), jnp.float32, smallest / len(cuts), largest / len(cuts))
        return jnp.repeat(jnp.exp(heights), shape[dim] // shards_of).reshape((-1,) + (1,) * (len(shape) - dim - 1))

    loudness = one(*cuts[0])
    for cut in cuts[1:]:
        loudness = loudness * one(*cut)
    return loudness


def normal_values(own_key, shape, spread, bound, shards=(), kind=jnp.bfloat16):
    level = steps_of(own_key, shape, shards, -0.22, 0.18) if shards else 1.0
    values = jax.random.normal(own_key, shape, jnp.float32) * spread * level
    return jnp.minimum(jnp.maximum(values, -bound), bound).astype(kind)


def setup_inputs(seed: int = 0) -> dict:
    key_list = jax.random.split(jax.random.key(seed), 7)
    field = normal_values(key_list[0], (NZ, NY, NX), 1.0, 6.0, ((0, 32), (1, 8)))
    tf_centers = jnp.clip(jax.random.uniform(key_list[1], (BUMPS,), jnp.float32, -1.5, 1.5), -1.5, 1.5)
    tf_widths = jnp.clip(jnp.exp(jax.random.uniform(key_list[2], (BUMPS,), jnp.float32, math.log(0.4), math.log(1.2))), 0.4, 1.2)
    tf_density = jnp.clip(jnp.exp(jax.random.uniform(key_list[3], (BUMPS,), jnp.float32, math.log(0.5), math.log(4.0))), 0.5, 4.0)
    tf_colors = jnp.clip(jax.random.uniform(key_list[4], (3, BUMPS), jnp.float32, 0.1, 1.0), 0.1, 1.0)
    light = jnp.clip(jax.random.uniform(key_list[5], (3,), jnp.float32, 0.5, 1.5), 0.5, 1.5)
    return {"field": field, "tf_centers": tf_centers, "tf_widths": tf_widths, "tf_density": tf_density, "tf_colors": tf_colors, "light": light}


def shade_cells(padded, tf_centers, tf_widths, tf_density, tf_colors, light, step_size):
    values = padded[1:-1, 1:-1, 1:-1]
    grad_z = (padded[2:, 1:-1, 1:-1] - padded[:-2, 1:-1, 1:-1]) * 0.5
    grad_y = (padded[1:-1, 2:, 1:-1] - padded[1:-1, :-2, 1:-1]) * 0.5
    grad_x = (padded[1:-1, 1:-1, 2:] - padded[1:-1, 1:-1, :-2]) * 0.5
    grad_sq = grad_z * grad_z + grad_y * grad_y + grad_x * grad_x
    light_dir = light / jnp.sqrt(jnp.sum(light * light))
    facing = jnp.abs(grad_z * light_dir[0] + grad_y * light_dir[1] + grad_x * light_dir[2])
    lighting = 0.3 + 0.7 * facing / jnp.sqrt(grad_sq + 1.0)
    sigma = jnp.zeros_like(values)
    bump_total = jnp.zeros_like(values)
    colour_red = jnp.zeros_like(values)
    colour_green = jnp.zeros_like(values)
    colour_blue = jnp.zeros_like(values)
    for bump_index in range(tf_centers.shape[0]):
        scaled = (values - tf_centers[bump_index]) / tf_widths[bump_index]
        bump = jnp.exp(-scaled * scaled)
        sigma = sigma + tf_density[bump_index] * bump
        bump_total = bump_total + bump
        colour_red = colour_red + tf_colors[0, bump_index] * bump
        colour_green = colour_green + tf_colors[1, bump_index] * bump
        colour_blue = colour_blue + tf_colors[2, bump_index] * bump
    factor = lighting / (bump_total + 0.1)
    emit = jnp.stack([colour_red * factor, colour_green * factor, colour_blue * factor], 0)
    depth_tau = sigma * (0.25 + grad_sq / (grad_sq + 1.0)) * step_size
    return (depth_tau, emit)

def compose_local(depth_tau, emit):
    before = jnp.cumsum(depth_tau, 0) - depth_tau
    weight_z = jnp.exp(-before) * (1.0 - jnp.exp(-depth_tau))
    colour_sum = lax.optimization_barrier(jnp.sum(weight_z[None] * emit, axis=1))
    return (colour_sum, lax.optimization_barrier(jnp.sum(depth_tau, 0)))

def reference(field, tf_centers, tf_widths, tf_density, tf_colors, light):
    padded = jnp.pad(field, 1)
    step_size = 0.5 / NZ
    band_count = NY // YD

    def one_band(band):
        start = (band * YD).astype(jnp.int32)
        piece = lax.dynamic_slice_in_dim(padded, start, YD + 2, 1).astype(jnp.float32)
        depth_tau, emit = shade_cells(piece, tf_centers, tf_widths, tf_density, tf_colors, light, step_size)
        colour_sum, tau_total = compose_local(depth_tau, emit)
        return jnp.concatenate([colour_sum, (1.0 - jnp.exp(-tau_total))[None]], 0)
    bands = lax.map(one_band, jnp.arange(band_count, dtype=jnp.int32))
    return jnp.transpose(bands, (1, 0, 2, 3)).reshape(4, NY, NX)
```

```python
import math

import jax
import jax.numpy as jnp
from jax import lax
from jax.experimental import pallas as pl
from jax.experimental.pallas import tpu as pltpu
from jax.sharding import PartitionSpec as P

LOG2E = math.log2(math.e)
TILE_ROWS = 16


def shade_kernel(
    step_size, centers, widths, density, colors, light,
    field, plane_lo, plane_hi, row_lo, row_hi,
    out, cells, slope_x, rays,
):
    depth, rows, width = field.shape
    lanes = width // 128

    lane = lax.broadcasted_iota(jnp.int32, (TILE_ROWS, 128), 1)

    def spread(plane, first, tile):
        for j in range(lanes):
            cells[j, plane, pl.ds(8 + first, TILE_ROWS), :] = tile[:, 128 * j : 128 * (j + 1)]

    def prepare(index, carry):
        plane = index // (rows // TILE_ROWS)
        first = pl.multiple_of((index % (rows // TILE_ROWS)) * TILE_ROWS, TILE_ROWS)
        tile = field[plane, pl.ds(first, TILE_ROWS), :].astype(jnp.float32)
        spread(plane + 1, first, tile)
        left = pltpu.roll(tile, 1, 1)
        right = pltpu.roll(tile, width - 1, 1)
        for j in range(lanes):
            before, after = left[:, 128 * j : 128 * (j + 1)], right[:, 128 * j : 128 * (j + 1)]
            if j == 0:
                before = jnp.where(lane == 0, 0.0, before)
            if j == lanes - 1:
                after = jnp.where(lane == 127, 0.0, after)
            slope_x[j, plane, pl.ds(first, TILE_ROWS), :] = after - before
        return carry

    lax.fori_loop(0, depth * (rows // TILE_ROWS), prepare, 0)
    for first in range(0, rows, TILE_ROWS):
        spread(0, first, plane_lo[first : first + TILE_ROWS, :].astype(jnp.float32))
        spread(depth + 1, first, plane_hi[first : first + TILE_ROWS, :].astype(jnp.float32))
    low, high = row_lo[...].astype(jnp.float32), row_hi[...].astype(jnp.float32)
    for j in range(lanes):
        for plane in range(depth):
            cells[j, plane + 1, 7:8, :] = low[plane : plane + 1, 128 * j : 128 * (j + 1)]
            cells[j, plane + 1, 8 + rows : 9 + rows, :] = high[plane : plane + 1, 128 * j : 128 * (j + 1)]

    def full(scalar):
        return jnp.full((TILE_ROWS, 128), scalar, jnp.float32)

    count = centers.shape[0]
    center = [full(centers[k]) for k in range(count)]
    sharp = [-LOG2E / (full(widths[k]) * full(widths[k])) for k in range(count)]
    dense = [full(density[k]) * (-4.0 * LOG2E * step_size) for k in range(count)]
    lights = [full(light[k]) for k in range(3)]
    length = lax.rsqrt(lights[0] * lights[0] + lights[1] * lights[1] + lights[2] * lights[2])
    lights = [component * length * 0.7 for component in lights]

    def march(index, carry):
        j = index // (rows // TILE_ROWS)
        first = (index % (rows // TILE_ROWS)) * TILE_ROWS
        here = pl.ds(pl.multiple_of(first + 8, 8), TILE_ROWS)
        previous, current = cells[j, 0, here, :], cells[j, 1, here, :]
        total = jnp.zeros((TILE_ROWS, 128), jnp.float32)
        clear = jnp.ones((TILE_ROWS, 128), jnp.float32)
        sums = [jnp.zeros((TILE_ROWS, 128), jnp.float32) for _ in range(count)]
        for plane in range(depth):
            following = cells[j, plane + 2, here, :]
            dz = following - previous
            dy = cells[j, plane + 1, pl.ds(first + 9, TILE_ROWS), :] - cells[j, plane + 1, pl.ds(first + 7, TILE_ROWS), :]
            dx = slope_x[j, plane, pl.ds(pl.multiple_of(first, TILE_ROWS), TILE_ROWS), :]
            root = lax.rsqrt(dz * dz + dy * dy + dx * dx + 4.0)
            lighting = 0.3 + jnp.abs(dz * lights[0] + dy * lights[1] + dx * lights[2]) * root
            bumps = []
            for k in range(count):
                offset = current - center[k]
                bumps.append(jnp.exp2(offset * offset * sharp[k]))
            sigma = dense[0] * bumps[0]
            weight = bumps[0] + 0.1
            for k in range(1, count):
                sigma = sigma + dense[k] * bumps[k]
                weight = weight + bumps[k]
            total = total + sigma * (0.3125 - root * root)
            remaining = jnp.exp2(total)
            factor = (clear - remaining) * lighting * pl.reciprocal(weight, approx=False)
            sums = [s + factor * b for s, b in zip(sums, bumps)]
            previous, current, clear = current, following, remaining
        kept = pl.ds(pl.multiple_of(first, TILE_ROWS), TILE_ROWS)
        for c in range(3):
            colour = colors[c, 0] * sums[0]
            for k in range(1, count):
                colour = colour + colors[c, k] * sums[k]
            rays[j, c, kept, :] = colour
        rays[j, 3, kept, :] = total
        return carry

    lax.fori_loop(0, lanes * (rows // TILE_ROWS), march, 0)

    def pack(j, carry):
        for c in range(4):
            tiles = [rays[j, c, 16 * q : 16 * (q + 1), :] for q in range(4)]
            for band in range(4):
                picked = None
                for q in range(4):
                    shift = (32 * (q - band)) % 128
                    moved = pltpu.roll(tiles[q], shift, 1) if shift else tiles[q]
                    picked = moved if q == 0 else jnp.where(lane >= 32 * q, moved, picked)
                out[4 * j + band, 16 * c : 16 * (c + 1), :] = picked
        return carry

    lax.fori_loop(0, lanes, pack, 0)


def compose_kernel(bricks, out):
    count = bricks.shape[0]
    total = jnp.zeros((16, 128), jnp.float32)
    image = [jnp.zeros((16, 128), jnp.float32) for _ in range(3)]
    for brick in range(count):
        front = jnp.exp2(total)
        for c in range(3):
            image[c] = image[c] + front * bricks[brick, 16 * c : 16 * (c + 1), :]
        total = total + bricks[brick, 48:64, :]
    image.append(1.0 - jnp.exp2(total))
    for c in range(4):
        turned = image[c].T
        out[c] = jnp.concatenate([turned[32 * q : 32 * (q + 1), :] for q in range(4)], axis=1)


def shards(field, tf_centers, tf_widths, tf_density, tf_colors, light):
    depth_count, row_count = lax.axis_size("depth"), lax.axis_size("rows")
    depth, rows, width = field.shape
    step_size = 0.5 / (depth * depth_count)

    def around(low_source, high_source, axis, count):
        up = [(i, i + 1) for i in range(count - 1)]
        down = [(i + 1, i) for i in range(count - 1)]
        return lax.ppermute(low_source, axis, up), lax.ppermute(high_source, axis, down)

    plane_lo, plane_hi = around(field[-1], field[0], "depth", depth_count)
    row_lo, row_hi = around(field[:, -1], field[:, 0], "rows", row_count)

    smem = pl.BlockSpec(memory_space=pltpu.SMEM)
    vmem = pl.BlockSpec(memory_space=pltpu.VMEM)
    lanes = width // 128
    bricks = pl.pallas_call(
        lambda *refs: shade_kernel(step_size, *refs),
        out_shape=jax.ShapeDtypeStruct((width // 32, rows, 128), jnp.float32),
        in_specs=[smem] * 5 + [vmem] * 5,
        out_specs=vmem,
        scratch_shapes=[
            pltpu.VMEM((lanes, depth + 2, rows + 16, 128), jnp.float32),
            pltpu.VMEM((lanes, depth, rows, 128), jnp.float32),
            pltpu.VMEM((lanes, 4, rows, 128), jnp.float32),
        ],
        compiler_params=pltpu.CompilerParams(vmem_limit_bytes=40 * 1024 * 1024),
        name="shade",
    )(tf_centers, tf_widths, tf_density, tf_colors, light, field, plane_lo, plane_hi, row_lo, row_hi)
    bricks = lax.all_to_all(bricks, "depth", 0, 0, tiled=True)
    image = pl.pallas_call(
        compose_kernel,
        out_shape=jax.ShapeDtypeStruct((4, width // depth_count, rows), jnp.float32),
        in_specs=[vmem],
        out_specs=vmem,
        name="compose",
    )(bricks)
    return jnp.transpose(image, (0, 2, 1))


def solution(mesh):
    placed = (P("depth", "rows", None), P(), P(), P(), P(), P())
    return jax.shard_map(
        shards, mesh=mesh, in_specs=placed, out_specs=P(None, "rows", "depth"), check_vma=False
    )
```

```python
import math

import jax
import jax.numpy as jnp
from jax import lax
from jax.experimental import pallas as pl
from jax.experimental.pallas import tpu as pltpu
from jax.sharding import PartitionSpec as P

LOG2E = math.log2(math.e)
TILE = 16
LANES = 128
BAND = 32
MB = 1024 * 1024


def dither(brick, shape):
    lane = lax.broadcasted_iota(jnp.int32, shape, 1)
    row = lax.broadcasted_iota(jnp.int32, shape, 0)
    phase = (lane * 29 + row * 13 + brick * 37) & 63
    return phase.astype(jnp.float32) * (1.0 / 64.0) + 1.0


def edges_kernel(field, first, last, row_first, row_last, tiles, gathered, sems):
    depth, rows, _ = field.shape
    copies = [
        pltpu.make_async_copy(field.at[:, 0:TILE], tiles.at[0], sems.at[0]),
        pltpu.make_async_copy(field.at[:, rows - TILE : rows], tiles.at[1], sems.at[1]),
        pltpu.make_async_copy(field.at[0], first, sems.at[2]),
        pltpu.make_async_copy(field.at[depth - 1], last, sems.at[3]),
    ]
    for copy in copies:
        copy.start()
    for side, (row, out) in enumerate(((0, row_first), (TILE - 1, row_last))):
        copies[side].wait()
        for plane in range(depth):
            tile = tiles[side, plane].astype(jnp.float32)
            gathered[side, plane : plane + 1, :] = tile[row : row + 1, :]
        out[...] = gathered[side].astype(jnp.bfloat16)
    copies[2].wait()
    copies[3].wait()


def shade_kernel(
    step_size, depth_count, row_count,
    centers_hbm, widths_hbm, density_hbm, colors_hbm, light_hbm, field_hbm,
    plane_lo, plane_hi, row_lo, row_hi,
    out, field, cells, rays, centers, widths, density, colors, light, field_sems, sems,
):
    depth, rows, width = field.shape
    lanes, tiles = width // LANES, rows // TILE

    chunks = field_sems.shape[0]
    chunk = depth // chunks
    loads = [
        pltpu.make_async_copy(
            field_hbm.at[pl.ds(c * chunk, chunk)], field.at[pl.ds(c * chunk, chunk)], field_sems.at[c]
        )
        for c in range(chunks)
    ]
    smalls = [
        pltpu.make_async_copy(source, target, sems.at[i])
        for i, (source, target) in enumerate(
            (
                (centers_hbm, centers), (widths_hbm, widths), (density_hbm, density),
                (colors_hbm, colors), (light_hbm, light),
            )
        )
    ]
    for copy in loads + smalls:
        copy.start()

    def spread(plane, first, tile):
        for j in range(lanes):
            cells[j + 1, plane, pl.ds(8 + first, TILE), :] = tile[:, LANES * j : LANES * (j + 1)]

    me, row_me = lax.axis_index("depth"), lax.axis_index("rows")
    keep_lo = (me > 0).astype(jnp.float32)
    keep_hi = (me < depth_count - 1).astype(jnp.float32)
    keep_up = (row_me > 0).astype(jnp.float32)
    keep_down = (row_me < row_count - 1).astype(jnp.float32)
    for first in range(0, rows, TILE):
        spread(0, first, plane_lo[first : first + TILE, :].astype(jnp.float32) * keep_lo)
        spread(depth + 1, first, plane_hi[first : first + TILE, :].astype(jnp.float32) * keep_hi)
    low, high = row_lo[...].astype(jnp.float32) * keep_up, row_hi[...].astype(jnp.float32) * keep_down
    for j in range(lanes):
        for plane in range(depth):
            cells[j + 1, plane + 1, 7:8, :] = low[plane : plane + 1, LANES * j : LANES * (j + 1)]
            cells[j + 1, plane + 1, 8 + rows : 9 + rows, :] = high[plane : plane + 1, LANES * j : LANES * (j + 1)]
    for side in (0, lanes + 1):
        for plane in range(depth):
            cells[side, plane + 1, 8 : 8 + rows, :] = jnp.zeros((rows, LANES), jnp.float32)

    def prepare(index, carry):
        plane = index // tiles
        first = pl.multiple_of((index % tiles) * TILE, TILE)
        spread(plane + 1, first, field[plane, pl.ds(first, TILE), :].astype(jnp.float32))
        return carry

    for c in range(chunks):
        loads[c].wait()
        lax.fori_loop(c * chunk * tiles, (c + 1) * chunk * tiles, prepare, 0)
    for copy in smalls:
        copy.wait()

    def full(scalar):
        return jnp.full((TILE, LANES), scalar, jnp.float32)

    count = centers.shape[0]
    center = [full(centers[k]) for k in range(count)]
    sharp = [-LOG2E / (full(widths[k]) * full(widths[k])) for k in range(count)]
    dense = [full(density[k]) * (-4.0 * LOG2E * step_size) for k in range(count)]
    lights = [full(light[k]) for k in range(3)]
    length = lax.rsqrt(lights[0] * lights[0] + lights[1] * lights[1] + lights[2] * lights[2])
    lights = [component * length * 0.7 for component in lights]

    lane = lax.broadcasted_iota(jnp.int32, (TILE, LANES), 1)
    at_first, at_last = lane == 0, lane == LANES - 1
    upper, odd = lane >= 64, (lane & 32) > 0
    scale = dither(me, (TILE, LANES)) * 65536.0

    def pack(j, c):
        def exchange(a, b, mask, shift):
            moved = pltpu.roll(jnp.where(mask, a, b), shift, 1)
            return jnp.where(mask, moved, a), jnp.where(mask, b, moved)

        part = [rays[j & 1, c, TILE * q : TILE * (q + 1), :] for q in range(4)]
        part[0], part[2] = exchange(part[0], part[2], upper, 64)
        part[1], part[3] = exchange(part[1], part[3], upper, 64)
        part[0], part[1] = exchange(part[0], part[1], odd, 32)
        part[2], part[3] = exchange(part[2], part[3], odd, 32)
        for band in range(4):
            value = part[band] * scale
            value = value * value
            value = value * value
            value = value * value
            out[4 * j + band, pl.ds(pl.multiple_of(TILE * c, TILE), TILE), :] = value.astype(jnp.bfloat16)

    def march(index, carry):
        j, tile = index // tiles, index % tiles
        first = tile * TILE
        here = pl.ds(pl.multiple_of(first + 8, 8), TILE)
        previous, current = cells[j + 1, 0, here, :], cells[j + 1, 1, here, :]
        total = jnp.zeros((TILE, LANES), jnp.float32)
        clear = jnp.ones((TILE, LANES), jnp.float32)
        sums = [jnp.zeros((TILE, LANES), jnp.float32) for _ in range(count)]
        for plane in range(depth):
            following = cells[j + 1, plane + 2, here, :]
            dz = following - previous
            dy = (
                cells[j + 1, plane + 1, pl.ds(first + 9, TILE), :]
                - cells[j + 1, plane + 1, pl.ds(first + 7, TILE), :]
            )
            dx = pltpu.roll(
                jnp.where(at_first, cells[j + 2, plane + 1, here, :], current), LANES - 1, 1
            ) - pltpu.roll(jnp.where(at_last, cells[j, plane + 1, here, :], current), 1, 1)
            root = lax.rsqrt(dz * dz + dy * dy + dx * dx + 4.0)
            lighting = 0.3 + jnp.abs(dz * lights[0] + dy * lights[1] + dx * lights[2]) * root
            bumps = []
            for k in range(count):
                offset = current - center[k]
                bumps.append(jnp.exp2(offset * offset * sharp[k]))
            sigma = dense[0] * bumps[0]
            weight = bumps[0] + 0.1
            for k in range(1, count):
                sigma = sigma + dense[k] * bumps[k]
                weight = weight + bumps[k]
            total = total + sigma * (0.3125 - root * root)
            remaining = jnp.exp2(total)
            factor = (clear - remaining) * lighting * pl.reciprocal(weight)
            sums = [s + factor * b for s, b in zip(sums, bumps)]
            previous, current, clear = current, following, remaining
        kept = pl.ds(pl.multiple_of(first, TILE), TILE)
        for c in range(3):
            colour = colors[c, 0] * sums[0]
            for k in range(1, count):
                colour = colour + colors[c, k] * sums[k]
            rays[j & 1, c, kept, :] = colour
        rays[j & 1, 3, kept, :] = -total
        pack(jnp.maximum(j - 1, 0), tile)
        return carry

    rays[...] = jnp.zeros_like(rays)
    lax.fori_loop(0, lanes * tiles, march, 0)
    for c in range(4):
        pack(lanes - 1, c)


def compose_kernel(bricks, out):
    count = bricks.shape[0]
    total = jnp.zeros((TILE, LANES), jnp.float32)
    image = [jnp.zeros((TILE, LANES), jnp.float32) for _ in range(3)]
    for brick in range(count):
        unscale = 1.0 / (dither(brick, (TILE, LANES)) * 65536.0)

        def value(c):
            coded = bricks[brick, TILE * c : TILE * (c + 1), :].astype(jnp.float32)
            return jnp.exp(jnp.log(coded) * 0.125) * unscale

        front = jnp.exp2(-total)
        for c in range(3):
            image[c] = image[c] + front * value(c)
        total = total + value(3)
    image.append(1.0 - jnp.exp2(-total))
    odd = (lax.axis_index("depth") & 1) == 1
    for c in range(4):
        turned = image[c].T
        block = [turned[BAND * q : BAND * (q + 1), :] for q in range(4)]
        block[0], block[2] = jnp.where(odd, block[2], block[0]), jnp.where(odd, block[0], block[2])
        out[c] = jnp.concatenate(block, axis=1)


def shards(field, tf_centers, tf_widths, tf_density, tf_colors, light):
    depth_count, row_count = lax.axis_size("depth"), lax.axis_size("rows")
    depth, rows, width = field.shape
    lanes = width // LANES
    step_size = 0.5 / (depth * depth_count)
    hbm, vmem = pl.BlockSpec(memory_space=pltpu.HBM), pl.BlockSpec(memory_space=pltpu.VMEM)

    edge = jax.ShapeDtypeStruct((rows, width), jnp.bfloat16)
    row_edge = jax.ShapeDtypeStruct((depth, width), jnp.bfloat16)
    first, last, row_first, row_last = pl.pallas_call(
        edges_kernel,
        out_shape=(edge, edge, row_edge, row_edge),
        in_specs=[hbm],
        out_specs=(vmem,) * 4,
        scratch_shapes=[
            pltpu.VMEM((2, depth, TILE, width), jnp.bfloat16),
            pltpu.VMEM((2, depth, width), jnp.float32),
            pltpu.SemaphoreType.DMA((4,)),
        ],
        compiler_params=pltpu.CompilerParams(vmem_limit_bytes=8 * MB),
        name="edges",
    )(field)

    def around(upward, downward, axis, count):
        up = [(i, (i + 1) % count) for i in range(count)]
        down = [((i + 1) % count, i) for i in range(count)]
        return lax.ppermute(upward, axis, up), lax.ppermute(downward, axis, down)

    plane_lo, plane_hi = around(last, first, "depth", depth_count)
    row_lo, row_hi = around(row_last, row_first, "rows", row_count)

    bricks = pl.pallas_call(
        lambda *refs: shade_kernel(step_size, depth_count, row_count, *refs),
        out_shape=jax.ShapeDtypeStruct((width // BAND, rows, LANES), jnp.bfloat16),
        in_specs=[hbm] * 6 + [vmem] * 4,
        out_specs=vmem,
        scratch_shapes=[
            pltpu.VMEM((depth, rows, width), jnp.bfloat16),
            pltpu.VMEM((lanes + 2, depth + 2, rows + 16, LANES), jnp.float32),
            pltpu.VMEM((2, 4, rows, LANES), jnp.float32),
            pltpu.SMEM(tf_centers.shape, jnp.float32),
            pltpu.SMEM(tf_widths.shape, jnp.float32),
            pltpu.SMEM(tf_density.shape, jnp.float32),
            pltpu.SMEM(tf_colors.shape, jnp.float32),
            pltpu.SMEM(light.shape, jnp.float32),
            pltpu.SemaphoreType.DMA((4,)),
            pltpu.SemaphoreType.DMA((5,)),
        ],
        compiler_params=pltpu.CompilerParams(vmem_limit_bytes=32 * MB),
        name="shade",
    )(tf_centers, tf_widths, tf_density, tf_colors, light, field, plane_lo, plane_hi, row_lo, row_hi)
    bricks = lax.all_to_all(bricks, "depth", 0, 0, tiled=True)
    image = pl.pallas_call(
        compose_kernel,
        out_shape=jax.ShapeDtypeStruct((4, width // depth_count, rows), jnp.float32),
        in_specs=[vmem],
        out_specs=vmem,
        name="compose",
    )(bricks)
    return jnp.transpose(image, (0, 2, 1))


def solution(mesh):
    placed = (P("depth", "rows", None), P(), P(), P(), P(), P())
    return jax.shard_map(
        shards, mesh=mesh, in_specs=placed, out_specs=P(None, "rows", "depth"), check_vma=False
    )
```

```python
import math

import jax
import jax.numpy as jnp
from jax import lax
from jax.experimental import pallas as pl
from jax.experimental.pallas import tpu as pltpu
from jax.sharding import PartitionSpec as P

LOG2E = math.log2(math.e)
TILE = 16
LANES = 128
BAND = 32
MB = 1024 * 1024


def dither(brick, shape):
    lane = lax.broadcasted_iota(jnp.int32, shape, 1)
    row = lax.broadcasted_iota(jnp.int32, shape, 0)
    phase = (lane * 29 + row * 13 + brick * 37) & 63
    return phase.astype(jnp.float32) * (1.0 / 64.0) + 1.0


def edges_kernel(field, first, last, row_first, row_last, tiles, gathered, sems):
    depth, rows, _ = field.shape
    copies = [
        pltpu.make_async_copy(field.at[:, 0:TILE], tiles.at[0], sems.at[0]),
        pltpu.make_async_copy(field.at[:, rows - TILE : rows], tiles.at[1], sems.at[1]),
        pltpu.make_async_copy(field.at[0], first, sems.at[2]),
        pltpu.make_async_copy(field.at[depth - 1], last, sems.at[3]),
    ]
    for copy in copies:
        copy.start()
    for side, (row, out) in enumerate(((0, row_first), (TILE - 1, row_last))):
        copies[side].wait()
        for plane in range(depth):
            tile = tiles[side, plane].astype(jnp.float32)
            gathered[side, plane : plane + 1, :] = tile[row : row + 1, :]
        out[...] = gathered[side].astype(jnp.bfloat16)
    copies[2].wait()
    copies[3].wait()


def start_params(sources, targets, sems):
    copies = [
        pltpu.make_async_copy(source, target, sems.at[i]) for i, (source, target) in enumerate(zip(sources, targets))
    ]
    for copy in copies:
        copy.start()
    return copies


def shader(step_size, cells, centers, widths, density, colors, light):
    def full(scalar):
        return jnp.full((8, LANES), scalar, jnp.float32)

    count = centers.shape[0]
    center = [full(centers[k]) for k in range(count)]
    sharp = [-LOG2E / (full(widths[k]) * full(widths[k])) for k in range(count)]
    dense = [full(density[k]) * (-4.0 * LOG2E * step_size) for k in range(count)]
    lights = [full(light[k]) for k in range(3)]
    length = lax.rsqrt(lights[0] * lights[0] + lights[1] * lights[1] + lights[2] * lights[2])
    lights = [component * length * 0.7 for component in lights]
    lane = lax.broadcasted_iota(jnp.int32, (8, LANES), 1)
    at_first, at_last = lane == 0, lane == LANES - 1

    def rows_at(start):
        return pl.ds(pl.multiple_of(start + 8, 8), 8)

    def enter(j, start, plane, total=None, sums=None):
        zero = jnp.zeros((8, LANES), jnp.float32)
        before, at = cells[j + 1, plane, rows_at(start), :], cells[j + 1, plane + 1, rows_at(start), :]
        if total is None:
            return [before, at, zero, jnp.ones((8, LANES), jnp.float32)] + [zero] * count
        return [before, at, total, jnp.exp2(total)] + sums

    def step(j, start, plane, state):
        previous, current, total, clear, *sums = state
        here = rows_at(start)
        following = cells[j + 1, plane + 2, here, :]
        dz = following - previous
        dy = cells[j + 1, plane + 1, pl.ds(start + 9, 8), :] - cells[j + 1, plane + 1, pl.ds(start + 7, 8), :]
        dx = pltpu.roll(
            jnp.where(at_first, cells[j + 2, plane + 1, here, :], current), LANES - 1, 1
        ) - pltpu.roll(jnp.where(at_last, cells[j, plane + 1, here, :], current), 1, 1)
        root = lax.rsqrt(dz * dz + dy * dy + dx * dx + 4.0)
        lighting = 0.3 + jnp.abs(dz * lights[0] + dy * lights[1] + dx * lights[2]) * root
        bumps = []
        for k in range(count):
            offset = current - center[k]
            bumps.append(jnp.exp2(offset * offset * sharp[k]))
        sigma = dense[0] * bumps[0]
        weight = bumps[0] + 0.1
        for k in range(1, count):
            sigma = sigma + dense[k] * bumps[k]
            weight = weight + bumps[k]
        total = total + sigma * (0.3125 - root * root)
        remaining = jnp.exp2(total)
        factor = (clear - remaining) * lighting * pl.reciprocal(weight)
        sums = [s + factor * b for s, b in zip(sums, bumps)]
        return [current, following, total, remaining] + sums

    def mix(sums):
        mixed = []
        for c in range(3):
            colour = colors[c, 0] * sums[0]
            for k in range(1, count):
                colour = colour + colors[c, k] * sums[k]
            mixed.append(colour)
        return mixed

    return enter, step, mix


def spread(cells, plane, first, tile):
    for j in range(tile.shape[1] // LANES):
        cells[j + 1, plane, pl.ds(8 + first, TILE), :] = tile[:, LANES * j : LANES * (j + 1)]


def interior_kernel(step_size, *refs):
    param_sources, field_hbm, out, field, cells, params, field_sems, sems = (
        refs[:5], refs[5], refs[6], refs[7], refs[8], refs[9:14], refs[14], refs[15],
    )
    depth, rows, width = field.shape
    lanes, tiles = width // LANES, rows // TILE
    chunks = field_sems.shape[0]
    chunk = depth // chunks
    loads = []
    for c in range(chunks):
        part = pl.ds(c * chunk, chunk)
        loads.append(pltpu.make_async_copy(field_hbm.at[part], field.at[part], field_sems.at[c]))
        loads[c].start()
    smalls = start_params(param_sources, params, sems)

    for side in (0, lanes + 1):
        for plane in range(1, depth - 1):
            cells[side, plane + 1, 8 : 8 + rows, :] = jnp.zeros((rows, LANES), jnp.float32)

    def prepare(index, carry):
        plane = index // tiles
        first = pl.multiple_of((index % tiles) * TILE, TILE)
        spread(cells, plane + 1, first, field[plane, pl.ds(first, TILE), :].astype(jnp.float32))
        return carry

    for c in range(chunks):
        loads[c].wait()
        lax.fori_loop(c * chunk * tiles, (c + 1) * chunk * tiles, prepare, 0)
    for copy in smalls:
        copy.wait()
    enter, step, mix = shader(step_size, cells, *params)

    def march(j, carry):
        done = []
        for pair in range((rows - 16) // 16):
            starts = [8 + 16 * pair, 16 + 16 * pair]
            states = [enter(j, start, 1) for start in starts]
            for plane in range(1, depth - 1):
                states = [step(j, start, plane, state) for start, state in zip(starts, states)]
            done += [(start - 8, mix(state[4:]) + [state[2]]) for start, state in zip(starts, states)]
        for start, values in done:
            for c in range(4):
                out[j, c, start : start + 8, :] = values[c]
        return carry

    lax.fori_loop(0, lanes, march, 0)


def border_kernel(step_size, depth_count, row_count, *refs):
    param_sources, field_hbm, plane_lo, plane_hi, row_lo, row_hi, inner, out = refs[:5], *refs[5:12]
    field, cells, rays, params, field_sems, sems = refs[12], refs[13], refs[14], refs[15:20], refs[20], refs[21]
    depth, rows, width = field.shape
    lanes = width // LANES
    parts = (
        (slice(0, depth), slice(0, TILE)),
        (slice(0, depth), slice(rows - TILE, rows)),
        (slice(0, 2), slice(TILE, rows - TILE)),
        (slice(depth - 2, depth), slice(TILE, rows - TILE)),
    )
    loads = []
    for c, part in enumerate(parts):
        loads.append(pltpu.make_async_copy(field_hbm.at[part], field.at[part], field_sems.at[c]))
        loads[c].start()
    smalls = start_params(param_sources, params, sems)

    me, row_me = lax.axis_index("depth"), lax.axis_index("rows")
    keep_lo = (me > 0).astype(jnp.float32)
    keep_hi = (me < depth_count - 1).astype(jnp.float32)
    keep_up = (row_me > 0).astype(jnp.float32)
    keep_down = (row_me < row_count - 1).astype(jnp.float32)
    for first in range(0, rows, TILE):
        spread(cells, 0, first, plane_lo[first : first + TILE, :].astype(jnp.float32) * keep_lo)
        spread(cells, depth + 1, first, plane_hi[first : first + TILE, :].astype(jnp.float32) * keep_hi)
    low, high = row_lo[...].astype(jnp.float32) * keep_up, row_hi[...].astype(jnp.float32) * keep_down
    for j in range(lanes):
        for plane in range(depth):
            cells[j + 1, plane + 1, 7:8, :] = low[plane : plane + 1, LANES * j : LANES * (j + 1)]
            cells[j + 1, plane + 1, 8 + rows : 9 + rows, :] = high[plane : plane + 1, LANES * j : LANES * (j + 1)]
    for side in (0, lanes + 1):
        for plane in range(depth):
            cells[side, plane + 1, 8 : 8 + rows, :] = jnp.zeros((rows, LANES), jnp.float32)

    for c, part in enumerate(parts):
        loads[c].wait()
        if c < 2:
            first = part[1].start

            def prepare(plane, carry, first=first):
                spread(cells, plane + 1, first, field[plane, first : first + TILE, :].astype(jnp.float32))
                return carry

            lax.fori_loop(0, depth, prepare, 0)
        else:
            for plane in range(part[0].start, part[0].stop):
                for first in range(TILE, rows - TILE, TILE):
                    spread(cells, plane + 1, first, field[plane, first : first + TILE, :].astype(jnp.float32))
    for copy in smalls:
        copy.wait()
    enter, step, mix = shader(step_size, cells, *params)

    lane = lax.broadcasted_iota(jnp.int32, (TILE, LANES), 1)
    upper, odd = lane >= 64, (lane & 32) > 0
    scale = dither(me, (TILE, LANES)) * 65536.0

    def pack(j, c):
        def exchange(a, b, mask, shift):
            moved = pltpu.roll(jnp.where(mask, a, b), shift, 1)
            return jnp.where(mask, moved, a), jnp.where(mask, b, moved)

        part = [rays[j & 1, c, TILE * q : TILE * (q + 1), :] for q in range(4)]
        part[0], part[2] = exchange(part[0], part[2], upper, 64)
        part[1], part[3] = exchange(part[1], part[3], upper, 64)
        part[0], part[1] = exchange(part[0], part[1], odd, 32)
        part[2], part[3] = exchange(part[2], part[3], odd, 32)
        for band in range(4):
            value = part[band] * scale
            value = value * value
            value = value * value
            value = value * value
            out[4 * j + band, TILE * c : TILE * (c + 1), :] = value.astype(jnp.bfloat16)

    def march(j, carry):
        for c in range(4):
            pack(jnp.maximum(j - 1, 0), c)
        done = []
        starts = [0, rows - 8]
        states = [enter(j, start, 0) for start in starts]
        for plane in range(depth):
            states = [step(j, start, plane, state) for start, state in zip(starts, states)]
        done += [(start, mix(state[4:]) + [state[2]]) for start, state in zip(starts, states)]
        for start in range(8, rows - 8, 8):
            state = step(j, start, 0, enter(j, start, 0))
            front, total = state[3], state[2] + inner[j, 3, start - 8 : start, :]
            state = step(j, start, depth - 1, enter(j, start, depth - 1, total, state[4:]))
            values = [v + front * inner[j, c, start - 8 : start, :] for c, v in enumerate(mix(state[4:]))]
            done.append((start, values + [state[2]]))
        for start, values in done:
            for c in range(3):
                rays[j & 1, c, start : start + 8, :] = values[c]
            rays[j & 1, 3, start : start + 8, :] = -values[3]
        return carry

    rays[...] = jnp.zeros_like(rays)
    lax.fori_loop(0, lanes, march, 0)
    for c in range(4):
        pack(lanes - 1, c)


def compose_kernel(bricks, out):
    count = bricks.shape[0]
    total = jnp.zeros((TILE, LANES), jnp.float32)
    image = [jnp.zeros((TILE, LANES), jnp.float32) for _ in range(3)]
    for brick in range(count):
        unscale = 1.0 / (dither(brick, (TILE, LANES)) * 65536.0)

        def value(c):
            coded = bricks[brick, TILE * c : TILE * (c + 1), :].astype(jnp.float32)
            return jnp.exp(jnp.log(coded) * 0.125) * unscale

        front = jnp.exp2(-total)
        for c in range(3):
            image[c] = image[c] + front * value(c)
        total = total + value(3)
    image.append(1.0 - jnp.exp2(-total))
    odd = (lax.axis_index("depth") & 1) == 1
    for c in range(4):
        turned = image[c].T
        block = [turned[BAND * q : BAND * (q + 1), :] for q in range(4)]
        block[0], block[2] = jnp.where(odd, block[2], block[0]), jnp.where(odd, block[0], block[2])
        out[c] = jnp.concatenate(block, axis=1)


def shards(field, tf_centers, tf_widths, tf_density, tf_colors, light):
    depth_count, row_count = lax.axis_size("depth"), lax.axis_size("rows")
    depth, rows, width = field.shape
    lanes = width // LANES
    step_size = 0.5 / (depth * depth_count)
    hbm, vmem = pl.BlockSpec(memory_space=pltpu.HBM), pl.BlockSpec(memory_space=pltpu.VMEM)

    edge = jax.ShapeDtypeStruct((rows, width), jnp.bfloat16)
    row_edge = jax.ShapeDtypeStruct((depth, width), jnp.bfloat16)
    first, last, row_first, row_last = pl.pallas_call(
        edges_kernel,
        out_shape=(edge, edge, row_edge, row_edge),
        in_specs=[hbm],
        out_specs=(vmem,) * 4,
        scratch_shapes=[
            pltpu.VMEM((2, depth, TILE, width), jnp.bfloat16),
            pltpu.VMEM((2, depth, width), jnp.float32),
            pltpu.SemaphoreType.DMA((4,)),
        ],
        compiler_params=pltpu.CompilerParams(vmem_limit_bytes=56 * MB),
        name="edges",
    )(field)

    inner_field, first, last, row_first, row_last = lax.optimization_barrier(
        (field, first, last, row_first, row_last)
    )

    def around(upward, downward, axis, count):
        up = [(i, (i + 1) % count) for i in range(count)]
        down = [((i + 1) % count, i) for i in range(count)]
        return lax.ppermute(upward, axis, up), lax.ppermute(downward, axis, down)

    plane_lo, plane_hi = around(last, first, "depth", depth_count)
    row_lo, row_hi = around(row_last, row_first, "rows", row_count)

    params = (tf_centers, tf_widths, tf_density, tf_colors, light)
    field_scratch = [
        pltpu.VMEM((depth, rows, width), jnp.bfloat16),
        pltpu.VMEM((lanes + 2, depth + 2, rows + 16, LANES), jnp.float32),
    ]
    param_scratch = [pltpu.SMEM(param.shape, jnp.float32) for param in params] + [
        pltpu.SemaphoreType.DMA((4,)),
        pltpu.SemaphoreType.DMA((5,)),
    ]
    inner = pl.pallas_call(
        lambda *refs: interior_kernel(step_size, *refs),
        out_shape=jax.ShapeDtypeStruct((lanes, 4, rows - 16, LANES), jnp.float32),
        in_specs=[hbm] * 6,
        out_specs=vmem,
        scratch_shapes=field_scratch + param_scratch,
        compiler_params=pltpu.CompilerParams(vmem_limit_bytes=32 * MB),
        cost_estimate=pl.CostEstimate(flops=60_000_000, bytes_accessed=3_000_000, transcendentals=5_000_000),
        name="interior",
    )(*params, inner_field)
    bricks = pl.pallas_call(
        lambda *refs: border_kernel(step_size, depth_count, row_count, *refs),
        out_shape=jax.ShapeDtypeStruct((width // BAND, rows, LANES), jnp.bfloat16),
        in_specs=[hbm] * 6 + [vmem] * 5,
        out_specs=vmem,
        scratch_shapes=field_scratch + [pltpu.VMEM((2, 4, rows, LANES), jnp.float32)] + param_scratch,
        compiler_params=pltpu.CompilerParams(vmem_limit_bytes=32 * MB),
        name="border",
    )(*params, field, plane_lo, plane_hi, row_lo, row_hi, inner)
    bricks = lax.all_to_all(bricks, "depth", 0, 0, tiled=True)
    image = pl.pallas_call(
        compose_kernel,
        out_shape=jax.ShapeDtypeStruct((4, width // depth_count, rows), jnp.float32),
        in_specs=[vmem],
        out_specs=vmem,
        compiler_params=pltpu.CompilerParams(vmem_limit_bytes=16 * MB),
        name="compose",
    )(bricks)
    return jnp.transpose(image, (0, 2, 1))


def solution(mesh):
    placed = (P("depth", "rows", None), P(), P(), P(), P(), P())
    return jax.shard_map(
        shards, mesh=mesh, in_specs=placed, out_specs=P(None, "rows", "depth"), check_vma=False
    )
```

```python
import math

import jax
import jax.numpy as jnp
from jax import lax
from jax.experimental import pallas as pl
from jax.experimental.pallas import tpu as pltpu
from jax.sharding import PartitionSpec as P

LOG2E = math.log2(math.e)
TILE = 16
LANES = 128
BAND = 32
MB = 1024 * 1024


def dither(brick, shape):
    lane = lax.broadcasted_iota(jnp.int32, shape, 1)
    row = lax.broadcasted_iota(jnp.int32, shape, 0)
    phase = (lane * 29 + row * 13 + brick * 37) & 63
    return phase.astype(jnp.float32) * (1.0 / 64.0) + 1.0


def edges_kernel(field, plane_one, plane_two, row_one, row_two, tiles, gathered, sems):
    depth, rows, _ = field.shape
    chosen = jnp.where((lax.axis_index("depth") & 1) == 0, depth - 1, 0)
    copies = [
        pltpu.make_async_copy(field.at[:, 0:TILE], tiles.at[0], sems.at[0]),
        pltpu.make_async_copy(field.at[:, rows - TILE : rows], tiles.at[1], sems.at[1]),
        pltpu.make_async_copy(field.at[chosen], plane_one, sems.at[2]),
        pltpu.make_async_copy(field.at[depth - 1 - chosen], plane_two, sems.at[3]),
    ]
    for copy in copies:
        copy.start()
    for side, row in ((0, 0), (1, TILE - 1)):
        copies[side].wait()
        for plane in range(depth):
            tile = tiles[side, plane].astype(jnp.float32)
            gathered[side, plane : plane + 1, :] = tile[row : row + 1, :]
    even = (lax.axis_index("rows") & 1) == 0
    row_one[...] = jnp.where(even, gathered[1], gathered[0]).astype(jnp.bfloat16)
    row_two[...] = jnp.where(even, gathered[0], gathered[1]).astype(jnp.bfloat16)
    copies[2].wait()
    copies[3].wait()


def start_params(sources, targets, sems):
    copies = [
        pltpu.make_async_copy(source, target, sems.at[i]) for i, (source, target) in enumerate(zip(sources, targets))
    ]
    for copy in copies:
        copy.start()
    return copies


def shader(step_size, cells, centers, widths, density, colors, light):
    def full(scalar):
        return jnp.full((8, LANES), scalar, jnp.float32)

    count = centers.shape[0]
    center = [full(centers[k]) for k in range(count)]
    sharp = [-LOG2E / (full(widths[k]) * full(widths[k])) for k in range(count)]
    dense = [full(density[k]) * (-4.0 * LOG2E * step_size) for k in range(count)]
    lights = [full(light[k]) for k in range(3)]
    length = lax.rsqrt(lights[0] * lights[0] + lights[1] * lights[1] + lights[2] * lights[2])
    lights = [component * length * 0.7 for component in lights]
    lane = lax.broadcasted_iota(jnp.int32, (8, LANES), 1)
    at_first, at_last = lane == 0, lane == LANES - 1

    def rows_at(start):
        return pl.ds(pl.multiple_of(start + 8, 8), 8)

    def enter(j, start, plane, total=None, sums=None):
        zero = jnp.zeros((8, LANES), jnp.float32)
        before, at = cells[j + 1, plane, rows_at(start), :], cells[j + 1, plane + 1, rows_at(start), :]
        if total is None:
            return [before, at, zero, jnp.ones((8, LANES), jnp.float32)] + [zero] * count
        return [before, at, total, jnp.exp2(total)] + sums

    def step(j, start, plane, state):
        previous, current, total, clear, *sums = state
        here = rows_at(start)
        following = cells[j + 1, plane + 2, here, :]
        dz = following - previous
        dy = cells[j + 1, plane + 1, pl.ds(start + 9, 8), :] - cells[j + 1, plane + 1, pl.ds(start + 7, 8), :]
        dx = pltpu.roll(
            jnp.where(at_first, cells[j + 2, plane + 1, here, :], current), LANES - 1, 1
        ) - pltpu.roll(jnp.where(at_last, cells[j, plane + 1, here, :], current), 1, 1)
        root = lax.rsqrt(dz * dz + dy * dy + dx * dx + 4.0)
        lighting = 0.3 + jnp.abs(dz * lights[0] + dy * lights[1] + dx * lights[2]) * root
        bumps = []
        for k in range(count):
            offset = current - center[k]
            bumps.append(jnp.exp2(offset * offset * sharp[k]))
        sigma = dense[0] * bumps[0]
        weight = bumps[0] + 0.1
        for k in range(1, count):
            sigma = sigma + dense[k] * bumps[k]
            weight = weight + bumps[k]
        total = total + sigma * (0.3125 - root * root)
        remaining = jnp.exp2(total)
        factor = (clear - remaining) * lighting * pl.reciprocal(weight)
        sums = [s + factor * b for s, b in zip(sums, bumps)]
        return [current, following, total, remaining] + sums

    def mix(sums):
        mixed = []
        for c in range(3):
            colour = colors[c, 0] * sums[0]
            for k in range(1, count):
                colour = colour + colors[c, k] * sums[k]
            mixed.append(colour)
        return mixed

    return enter, step, mix


def spread(cells, plane, first, tile):
    for j in range(tile.shape[1] // LANES):
        cells[j + 1, plane, pl.ds(8 + first, TILE), :] = tile[:, LANES * j : LANES * (j + 1)]


def interior_kernel(step_size, *refs):
    param_sources, field, out, cells, params, sems = refs[:5], refs[5], refs[6], refs[7], refs[8:13], refs[13]
    depth, rows, width = field.shape
    lanes, tiles = width // LANES, rows // TILE
    smalls = start_params(param_sources, params, sems)

    for side in (0, lanes + 1):
        for plane in range(1, depth - 1):
            cells[side, plane + 1, 8 : 8 + rows, :] = jnp.zeros((rows, LANES), jnp.float32)

    def prepare(index, carry):
        plane = index // tiles
        first = pl.multiple_of((index % tiles) * TILE, TILE)
        spread(cells, plane + 1, first, field[plane, pl.ds(first, TILE), :].astype(jnp.float32))
        return carry

    lax.fori_loop(0, depth * tiles, prepare, 0)
    for copy in smalls:
        copy.wait()
    enter, step, mix = shader(step_size, cells, *params)

    def march(j, carry):
        done = []
        for pair in range((rows - 16) // 16):
            starts = [8 + 16 * pair, 16 + 16 * pair]
            states = [enter(j, start, 1) for start in starts]
            for plane in range(1, depth - 1):
                states = [step(j, start, plane, state) for start, state in zip(starts, states)]
            done += [(start - 8, mix(state[4:]) + [state[2]]) for start, state in zip(starts, states)]
        for start, values in done:
            for c in range(4):
                out[j, c, start : start + 8, :] = values[c]
        return carry

    lax.fori_loop(0, lanes, march, 0)


def border_kernel(step_size, depth_count, row_count, *refs):
    param_sources, field, plane_one, plane_two, row_one, row_two, inner, out = refs[:5], *refs[5:12]
    cells, rays, params, sems = refs[12], refs[13], refs[14:19], refs[19]
    depth, rows, width = field.shape
    lanes = width // LANES
    smalls = start_params(param_sources, params, sems)

    def sided(index, count):
        even = (index & 1) == 0
        return even, (index > 0).astype(jnp.float32), (index < count - 1).astype(jnp.float32)

    def around(one, two, even, keep_lo, keep_hi):
        one, two = one.astype(jnp.float32), two.astype(jnp.float32)
        return jnp.where(even, two, one) * keep_lo, jnp.where(even, one, two) * keep_hi

    me = lax.axis_index("depth")
    plane_sides, row_sides = sided(me, depth_count), sided(lax.axis_index("rows"), row_count)
    for first in range(0, rows, TILE):
        part = pl.ds(first, TILE)
        low, high = around(plane_one[part, :], plane_two[part, :], *plane_sides)
        spread(cells, 0, first, low)
        spread(cells, depth + 1, first, high)
    low, high = around(row_one[...], row_two[...], *row_sides)
    for j in range(lanes):
        for plane in range(depth):
            cells[j + 1, plane + 1, 7:8, :] = low[plane : plane + 1, LANES * j : LANES * (j + 1)]
            cells[j + 1, plane + 1, 8 + rows : 9 + rows, :] = high[plane : plane + 1, LANES * j : LANES * (j + 1)]
    for side in (0, lanes + 1):
        for plane in range(depth):
            cells[side, plane + 1, 8 : 8 + rows, :] = jnp.zeros((rows, LANES), jnp.float32)

    def prepare(plane, carry):
        for first in (0, rows - TILE):
            spread(cells, plane + 1, first, field[plane, first : first + TILE, :].astype(jnp.float32))
        return carry

    lax.fori_loop(0, depth, prepare, 0)
    for plane in (0, 1, depth - 2, depth - 1):
        for first in range(TILE, rows - TILE, TILE):
            spread(cells, plane + 1, first, field[plane, first : first + TILE, :].astype(jnp.float32))
    for copy in smalls:
        copy.wait()
    enter, step, mix = shader(step_size, cells, *params)

    lane = lax.broadcasted_iota(jnp.int32, (TILE, LANES), 1)
    upper, odd = lane >= 64, (lane & 32) > 0
    scale = dither(me, (TILE, LANES)) * 65536.0

    def pack(j, c):
        def exchange(a, b, mask, shift):
            moved = pltpu.roll(jnp.where(mask, a, b), shift, 1)
            return jnp.where(mask, moved, a), jnp.where(mask, b, moved)

        part = [rays[j & 1, c, TILE * q : TILE * (q + 1), :] for q in range(4)]
        part[0], part[2] = exchange(part[0], part[2], upper, 64)
        part[1], part[3] = exchange(part[1], part[3], upper, 64)
        part[0], part[1] = exchange(part[0], part[1], odd, 32)
        part[2], part[3] = exchange(part[2], part[3], odd, 32)
        for band in range(4):
            value = part[band] * scale
            value = value * value
            value = value * value
            value = value * value
            out[4 * j + band, TILE * c : TILE * (c + 1), :] = value.astype(jnp.bfloat16)

    def march(j, carry):
        for c in range(4):
            pack(jnp.maximum(j - 1, 0), c)
        done = []
        starts = [0, rows - 8]
        states = [enter(j, start, 0) for start in starts]
        for plane in range(depth):
            states = [step(j, start, plane, state) for start, state in zip(starts, states)]
        done += [(start, mix(state[4:]) + [state[2]]) for start, state in zip(starts, states)]
        for start in range(8, rows - 8, 8):
            state = step(j, start, 0, enter(j, start, 0))
            front, total = state[3], state[2] + inner[j, 3, start - 8 : start, :]
            state = step(j, start, depth - 1, enter(j, start, depth - 1, total, state[4:]))
            values = [v + front * inner[j, c, start - 8 : start, :] for c, v in enumerate(mix(state[4:]))]
            done.append((start, values + [state[2]]))
        for start, values in done:
            for c in range(3):
                rays[j & 1, c, start : start + 8, :] = values[c]
            rays[j & 1, 3, start : start + 8, :] = -values[3]
        return carry

    rays[...] = jnp.zeros_like(rays)
    lax.fori_loop(0, lanes, march, 0)
    for c in range(4):
        pack(lanes - 1, c)


def compose_kernel(bricks, out):
    count = bricks.shape[0]
    total = jnp.zeros((TILE, LANES), jnp.float32)
    image = [jnp.zeros((TILE, LANES), jnp.float32) for _ in range(3)]
    for brick in range(count):
        unscale = 1.0 / (dither(brick, (TILE, LANES)) * 65536.0)

        def value(c):
            coded = bricks[brick, TILE * c : TILE * (c + 1), :].astype(jnp.float32)
            return jnp.exp(jnp.log(coded) * 0.125) * unscale

        front = jnp.exp2(-total)
        for c in range(3):
            image[c] = image[c] + front * value(c)
        total = total + value(3)
    image.append(1.0 - jnp.exp2(-total))
    odd = (lax.axis_index("depth") & 1) == 1
    for c in range(4):
        turned = image[c].T
        block = [turned[BAND * q : BAND * (q + 1), :] for q in range(4)]
        block[0], block[2] = jnp.where(odd, block[2], block[0]), jnp.where(odd, block[0], block[2])
        out[c] = jnp.concatenate(block, axis=1)


def shards(field, tf_centers, tf_widths, tf_density, tf_colors, light):
    depth_count, row_count = lax.axis_size("depth"), lax.axis_size("rows")
    depth, rows, width = field.shape
    lanes = width // LANES
    step_size = 0.5 / (depth * depth_count)
    hbm, vmem = pl.BlockSpec(memory_space=pltpu.HBM), pl.BlockSpec(memory_space=pltpu.VMEM)

    edge = jax.ShapeDtypeStruct((rows, width), jnp.bfloat16)
    row_edge = jax.ShapeDtypeStruct((depth, width), jnp.bfloat16)
    edges = pl.pallas_call(
        edges_kernel,
        out_shape=(edge, edge, row_edge, row_edge),
        in_specs=[hbm],
        out_specs=(vmem,) * 4,
        scratch_shapes=[
            pltpu.VMEM((2, depth, TILE, width), jnp.bfloat16),
            pltpu.VMEM((2, depth, width), jnp.float32),
            pltpu.SemaphoreType.DMA((4,)),
        ],
        compiler_params=pltpu.CompilerParams(vmem_limit_bytes=52 * MB),
        name="edges",
    )(field)

    inner_field, *edges = lax.optimization_barrier((field, *edges))

    def exchange(one, two, axis, count):
        near = [(k, k ^ 1) for k in range(count)]
        far = [(k, (k - 1 + 2 * (k & 1)) % count) for k in range(count)]
        return lax.ppermute(one, axis, near), lax.ppermute(two, axis, far)

    plane_one, plane_two = exchange(edges[0], edges[1], "depth", depth_count)
    row_one, row_two = exchange(edges[2], edges[3], "rows", row_count)

    params = (tf_centers, tf_widths, tf_density, tf_colors, light)
    cells = pltpu.VMEM((lanes + 2, depth + 2, rows + 16, LANES), jnp.float32)
    param_scratch = [pltpu.SMEM(param.shape, jnp.float32) for param in params] + [pltpu.SemaphoreType.DMA((5,))]
    inner = pl.pallas_call(
        lambda *refs: interior_kernel(step_size, *refs),
        out_shape=jax.ShapeDtypeStruct((lanes, 4, rows - 16, LANES), jnp.float32),
        in_specs=[hbm] * 5 + [vmem],
        out_specs=vmem,
        scratch_shapes=[cells] + param_scratch,
        compiler_params=pltpu.CompilerParams(vmem_limit_bytes=32 * MB),
        cost_estimate=pl.CostEstimate(flops=60_000_000, bytes_accessed=3_000_000, transcendentals=5_000_000),
        name="interior",
    )(*params, inner_field)
    bricks = pl.pallas_call(
        lambda *refs: border_kernel(step_size, depth_count, row_count, *refs),
        out_shape=jax.ShapeDtypeStruct((width // BAND, rows, LANES), jnp.bfloat16),
        in_specs=[hbm] * 5 + [vmem] * 6,
        out_specs=vmem,
        scratch_shapes=[cells, pltpu.VMEM((2, 4, rows, LANES), jnp.float32)] + param_scratch,
        compiler_params=pltpu.CompilerParams(vmem_limit_bytes=32 * MB),
        name="border",
    )(*params, field, plane_one, plane_two, row_one, row_two, inner)
    bricks = lax.all_to_all(bricks, "depth", 0, 0, tiled=True)
    image = pl.pallas_call(
        compose_kernel,
        out_shape=jax.ShapeDtypeStruct((4, width // depth_count, rows), jnp.float32),
        in_specs=[vmem],
        out_specs=vmem,
        compiler_params=pltpu.CompilerParams(vmem_limit_bytes=16 * MB),
        name="compose",
    )(bricks)
    return jnp.transpose(image, (0, 2, 1))


def solution(mesh):
    placed = (P("depth", "rows", None), P(), P(), P(), P(), P())
    return jax.shard_map(
        shards, mesh=mesh, in_specs=placed, out_specs=P(None, "rows", "depth"), check_vma=False
    )
```

```python
import math

import jax
import jax.numpy as jnp
from jax import lax
from jax.experimental import pallas as pl
from jax.experimental.pallas import tpu as pltpu
from jax.sharding import PartitionSpec as P

LOG2E = math.log2(math.e)
TILE = 16
LANES = 128
BAND = 32
MB = 1024 * 1024


def dither(brick, shape):
    lane = lax.broadcasted_iota(jnp.int32, shape, 1)
    row = lax.broadcasted_iota(jnp.int32, shape, 0)
    phase = (lane * 29 + row * 13 + brick * 37) & 63
    return phase.astype(jnp.float32) * (1.0 / 64.0) + 1.0


def edges_kernel(field, plane_one, plane_two, row_one, row_two, tiles, gathered, sems):
    depth, rows, _ = field.shape
    chosen = jnp.where((lax.axis_index("depth") & 1) == 0, depth - 1, 0)
    copies = [
        pltpu.make_async_copy(field.at[:, 0:TILE], tiles.at[0], sems.at[0]),
        pltpu.make_async_copy(field.at[:, rows - TILE : rows], tiles.at[1], sems.at[1]),
        pltpu.make_async_copy(field.at[chosen], plane_one, sems.at[2]),
        pltpu.make_async_copy(field.at[depth - 1 - chosen], plane_two, sems.at[3]),
    ]
    for copy in copies:
        copy.start()
    for side, row in ((0, 0), (1, TILE - 1)):
        copies[side].wait()
        for plane in range(depth):
            tile = tiles[side, plane].astype(jnp.float32)
            gathered[side, plane : plane + 1, :] = tile[row : row + 1, :]
    even = (lax.axis_index("rows") & 1) == 0
    row_one[...] = jnp.where(even, gathered[1], gathered[0]).astype(jnp.bfloat16)
    row_two[...] = jnp.where(even, gathered[0], gathered[1]).astype(jnp.bfloat16)
    copies[2].wait()
    copies[3].wait()


def start_params(sources, targets, sems):
    copies = [
        pltpu.make_async_copy(source, target, sems.at[i]) for i, (source, target) in enumerate(zip(sources, targets))
    ]
    for copy in copies:
        copy.start()
    return copies


def shader(step_size, cells, centers, widths, density, colors, light):
    def full(scalar):
        return jnp.full((8, LANES), scalar, jnp.float32)

    count = centers.shape[0]
    center = [full(centers[k]) for k in range(count)]
    sharp = [-LOG2E / (full(widths[k]) * full(widths[k])) for k in range(count)]
    dense = [full(density[k]) * (-4.0 * LOG2E * step_size) for k in range(count)]
    lights = [full(light[k]) for k in range(3)]
    length = lax.rsqrt(lights[0] * lights[0] + lights[1] * lights[1] + lights[2] * lights[2])
    lights = [component * length * 0.7 for component in lights]
    lane = lax.broadcasted_iota(jnp.int32, (8, LANES), 1)
    at_first, at_last = lane == 0, lane == LANES - 1

    def rows_at(start):
        return pl.ds(pl.multiple_of(start + 8, 8), 8)

    def enter(j, start, plane, total=None, sums=None):
        zero = jnp.zeros((8, LANES), jnp.float32)
        before, at = cells[j + 1, plane, rows_at(start), :], cells[j + 1, plane + 1, rows_at(start), :]
        if total is None:
            return [before, at, zero, jnp.ones((8, LANES), jnp.float32)] + [zero] * count
        return [before, at, total, jnp.exp2(total)] + sums

    def step(j, start, plane, state):
        previous, current, total, clear, *sums = state
        here = rows_at(start)
        following = cells[j + 1, plane + 2, here, :]
        dz = following - previous
        dy = cells[j + 1, plane + 1, pl.ds(start + 9, 8), :] - cells[j + 1, plane + 1, pl.ds(start + 7, 8), :]
        dx = pltpu.roll(
            jnp.where(at_first, cells[j + 2, plane + 1, here, :], current), LANES - 1, 1
        ) - pltpu.roll(jnp.where(at_last, cells[j, plane + 1, here, :], current), 1, 1)
        root = lax.rsqrt(dz * dz + dy * dy + dx * dx + 4.0)
        lighting = 0.3 + jnp.abs(dz * lights[0] + dy * lights[1] + dx * lights[2]) * root
        bumps = []
        for k in range(count):
            offset = current - center[k]
            bumps.append(jnp.exp2(offset * offset * sharp[k]))
        sigma = dense[0] * bumps[0]
        weight = bumps[0] + 0.1
        for k in range(1, count):
            sigma = sigma + dense[k] * bumps[k]
            weight = weight + bumps[k]
        total = total + sigma * (0.3125 - root * root)
        remaining = jnp.exp2(total)
        factor = (clear - remaining) * lighting * pl.reciprocal(weight)
        sums = [s + factor * b for s, b in zip(sums, bumps)]
        return [current, following, total, remaining] + sums

    def mix(sums):
        mixed = []
        for c in range(3):
            colour = colors[c, 0] * sums[0]
            for k in range(1, count):
                colour = colour + colors[c, k] * sums[k]
            mixed.append(colour)
        return mixed

    return enter, step, mix


def spread(cells, plane, first, tile):
    for j in range(tile.shape[1] // LANES):
        cells[j + 1, plane, pl.ds(pl.multiple_of(8 + first, 8), TILE), :] = tile[:, LANES * j : LANES * (j + 1)]


def is_even(axis):
    return (lax.axis_index(axis) & 1) == 0


def strips_of(upper_half, rows):
    outer = jnp.where(upper_half, 0, rows - 8)
    inner = jnp.where(upper_half, 8, rows // 2)
    return [outer] + [inner + 8 * i for i in range(rows // 16 - 1)]


def tiles_of(upper_half, rows):
    base = jnp.where(upper_half, 0, rows // 2 - TILE)
    return [base + TILE * i for i in range(rows // 2 // TILE + 1)]


def zero_sides(cells, upper_half, depth, rows, lanes):
    half = pl.ds(pl.multiple_of(8 + jnp.where(upper_half, 0, rows // 2), 8), rows // 2)
    for side in (0, lanes + 1):
        for plane in range(depth):
            cells[side, plane + 1, half, :] = jnp.zeros((rows // 2, LANES), jnp.float32)


def load_tile(field, cells, plane, first):
    part = field[plane, pl.ds(pl.multiple_of(first, TILE), TILE), :]
    spread(cells, plane + 1, first, part.astype(jnp.float32))


def load_halos(
    cells, plane_one, plane_two, row_one, row_two, upper_half, depth_count, row_count, depth, rows, lanes
):
    def sided(axis, count):
        index = lax.axis_index(axis)
        return is_even(axis), (index > 0).astype(jnp.float32), (index < count - 1).astype(jnp.float32)

    def around(one, two, even, keep_lo, keep_hi):
        one, two = one.astype(jnp.float32), two.astype(jnp.float32)
        return jnp.where(even, two, one) * keep_lo, jnp.where(even, one, two) * keep_hi

    plane_sides, row_sides = sided("depth", depth_count), sided("rows", row_count)
    for first in tiles_of(upper_half, rows):
        part = pl.ds(pl.multiple_of(first, TILE), TILE)
        low, high = around(plane_one[part, :], plane_two[part, :], *plane_sides)
        spread(cells, 0, first, low)
        spread(cells, depth + 1, first, high)
    low, high = around(row_one[...], row_two[...], *row_sides)
    beside, line = jnp.where(upper_half, low, high), pl.ds(jnp.where(upper_half, 7, 8 + rows), 1)
    for j in range(lanes):
        for plane in range(depth):
            cells[j + 1, plane + 1, line, :] = beside[plane : plane + 1, LANES * j : LANES * (j + 1)]


def encode(value, scale):
    value = value * scale
    value = value * value
    value = value * value
    return (value * value).astype(jnp.bfloat16)


def decode(coded, unscale):
    return jnp.exp(jnp.log(coded.astype(jnp.float32)) * 0.125) * unscale


def early_kernel(step_size, *refs):
    param_sources, field, out, cells, params, sems = refs[:5], refs[5], refs[6], refs[7], refs[8:13], refs[13]
    depth, rows, width = field.shape
    lanes = width // LANES
    smalls = start_params(param_sources, params, sems)
    send_upper = jnp.logical_not(is_even("depth"))
    zero_sides(cells, send_upper, depth, rows, lanes)
    firsts = tiles_of(send_upper, rows)

    def prepare(plane, carry):
        for first in firsts:
            load_tile(field, cells, plane, first)
        return carry

    lax.fori_loop(0, depth, prepare, 0)
    for copy in smalls:
        copy.wait()
    enter, step, mix = shader(step_size, cells, *params)
    starts = strips_of(send_upper, rows)[1:]

    def march(j, carry):
        states = [enter(j, start, 1) for start in starts]
        for plane in range(1, depth - 1):
            states = [step(j, start, plane, state) for start, state in zip(starts, states)]
        for i, state in enumerate(states):
            for c, value in enumerate(mix(state[4:]) + [state[2]]):
                out[j, c, 8 * i : 8 * i + 8, :] = value
        return carry

    lax.fori_loop(0, lanes, march, 0)


def send_kernel(step_size, depth_count, row_count, *refs):
    param_sources, field, plane_one, plane_two, row_one, row_two, early, out = refs[:5], *refs[5:12]
    cells, params, sems = refs[12], refs[13:18], refs[18]
    depth, rows, width = field.shape
    lanes = width // LANES
    smalls = start_params(param_sources, params, sems)
    send_upper = jnp.logical_not(is_even("depth"))
    zero_sides(cells, send_upper, depth, rows, lanes)
    firsts = tiles_of(send_upper, rows)
    load_halos(cells, plane_one, plane_two, row_one, row_two, send_upper, depth_count, row_count, depth, rows, lanes)
    outer = jnp.where(send_upper, 0, rows - TILE)

    def prepare(plane, carry):
        load_tile(field, cells, plane, outer)
        return carry

    lax.fori_loop(0, depth, prepare, 0)
    for plane in (0, 1, depth - 2, depth - 1):
        for first in firsts:
            load_tile(field, cells, plane, first)
    for copy in smalls:
        copy.wait()
    enter, step, mix = shader(step_size, cells, *params)
    starts = strips_of(send_upper, rows)
    scale = dither(lax.axis_index("depth"), (TILE, LANES)) * 65536.0

    def march(j, carry):
        state = enter(j, starts[0], 0)
        for plane in range(depth):
            state = step(j, starts[0], plane, state)
        strips = [mix(state[4:]) + [-state[2]]]
        for i, start in enumerate(starts[1:]):
            state = step(j, start, 0, enter(j, start, 0))
            front, total = state[3], state[2] + early[j, 3, 8 * i : 8 * i + 8, :]
            state = step(j, start, depth - 1, enter(j, start, depth - 1, total, state[4:]))
            values = [v + front * early[j, c, 8 * i : 8 * i + 8, :] for c, v in enumerate(mix(state[4:]))]
            strips.append(values + [-state[2]])
        for c in range(4):
            for i in range(0, len(strips), 2):
                both = jnp.concatenate([strips[i][c], strips[i + 1][c]], axis=0)
                out[j, c, 8 * i : 8 * i + 16, :] = encode(both, scale)
        return carry

    lax.fori_loop(0, lanes, march, 0)


def keep_kernel(step_size, depth_count, row_count, *refs):
    param_sources, field, plane_one, plane_two, row_one, row_two, out = refs[:5], *refs[5:11]
    cells, params, sems = refs[11], refs[12:17], refs[17]
    depth, rows, width = field.shape
    lanes = width // LANES
    smalls = start_params(param_sources, params, sems)
    keep_upper = is_even("depth")
    zero_sides(cells, keep_upper, depth, rows, lanes)
    firsts = tiles_of(keep_upper, rows)
    load_halos(cells, plane_one, plane_two, row_one, row_two, keep_upper, depth_count, row_count, depth, rows, lanes)

    def prepare(plane, carry):
        for first in firsts:
            load_tile(field, cells, plane, first)
        return carry

    lax.fori_loop(0, depth, prepare, 0)
    for copy in smalls:
        copy.wait()
    enter, step, mix = shader(step_size, cells, *params)
    starts = strips_of(keep_upper, rows)

    def march(j, carry):
        done = []
        for i in range(0, len(starts), 2):
            pair = starts[i : i + 2]
            states = [enter(j, start, 0) for start in pair]
            for plane in range(depth):
                states = [step(j, start, plane, state) for start, state in zip(pair, states)]
            done += [mix(state[4:]) + [-state[2]] for state in states]
        for i, values in enumerate(done):
            for c in range(4):
                out[j, c, 8 * i : 8 * i + 8, :] = values[c]
        return carry

    lax.fori_loop(0, lanes, march, 0)


def join_kernel(own, other, out):
    lanes = own.shape[0]
    me, even = lax.axis_index("depth"), is_even("depth")
    unscale = 1.0 / (dither(me + 1 - 2 * (me & 1), (TILE, LANES)) * 65536.0)
    scale = dither(me, (TILE, LANES)) * 32768.0
    lane = lax.broadcasted_iota(jnp.int32, (8, LANES), 1)
    upper, odd = lane >= 64, (lane & BAND) > 0

    def exchange(a, b, mask, shift):
        moved = pltpu.roll(jnp.where(mask, a, b), shift, 1)
        return jnp.where(mask, moved, a), jnp.where(mask, b, moved)

    def one(j):
        bands = [[], [], [], []]
        joined = [[] for _ in range(4)]
        for half in range(2):
            part = slice(TILE * half, TILE * (half + 1))
            mine = [own[j, c, part, :] for c in range(4)]
            theirs = [decode(other[j, c, part, :], unscale) for c in range(4)]
            front = jnp.exp2(-jnp.where(even, mine[3], theirs[3]))
            for c in range(3):
                first, second = jnp.where(even, mine[c], theirs[c]), jnp.where(even, theirs[c], mine[c])
                joined[c].append(first + front * second)
            joined[3].append(mine[3] + theirs[3])
        for c in range(4):
            strip = [joined[c][i // 2][8 * (i % 2) : 8 * (i % 2) + 8, :] for i in range(4)]
            strip[0], strip[2] = exchange(strip[0], strip[2], upper, 64)
            strip[1], strip[3] = exchange(strip[1], strip[3], upper, 64)
            strip[0], strip[1] = exchange(strip[0], strip[1], odd, BAND)
            strip[2], strip[3] = exchange(strip[2], strip[3], odd, BAND)
            for band in range(4):
                bands[band].append(strip[band])
        for band in range(4):
            for c in (0, 2):
                both = jnp.concatenate([bands[band][c], bands[band][c + 1]], axis=0)
                out[4 * j + band, 8 * c : 8 * c + 16, :] = encode(both, scale)

    for j in range(lanes):
        one(j)


def compose_kernel(bricks, out):
    count = bricks.shape[0]
    halves = []
    for half in range(2):
        total = jnp.zeros((8, LANES), jnp.float32)
        image = [jnp.zeros((8, LANES), jnp.float32) for _ in range(3)]
        for brick in range(half, count, 2):
            unscale = 1.0 / (dither(brick, (TILE, LANES)) * 32768.0)
            values = []
            for c in (0, 2):
                both = decode(bricks[brick, 8 * c : 8 * c + 16, :], unscale)
                values += [both[:8], both[8:]]
            front = jnp.exp2(-total)
            image = [sofar + front * value for sofar, value in zip(image, values)]
            total = total + values[3]
        halves.append(image + [1.0 - jnp.exp2(-total)])
    odd = jnp.logical_not(is_even("depth"))
    for c in range(4):
        turned = jnp.concatenate([halves[0][c], halves[1][c]], axis=0).T
        block = [turned[BAND * q : BAND * (q + 1), :] for q in range(4)]
        block[0], block[2] = jnp.where(odd, block[2], block[0]), jnp.where(odd, block[0], block[2])
        out[c] = jnp.concatenate(
            [block[q][:, :8] for q in (0, 1, 2, 3)] + [block[q][:, 8:] for q in (1, 2, 3, 0)], axis=1
        )


def shards(field, tf_centers, tf_widths, tf_density, tf_colors, light):
    depth_count, row_count = lax.axis_size("depth"), lax.axis_size("rows")
    depth, rows, width = field.shape
    lanes = width // LANES
    step_size = 0.5 / (depth * depth_count)
    hbm, vmem = pl.BlockSpec(memory_space=pltpu.HBM), pl.BlockSpec(memory_space=pltpu.VMEM)

    edge = jax.ShapeDtypeStruct((rows, width), jnp.bfloat16)
    row_edge = jax.ShapeDtypeStruct((depth, width), jnp.bfloat16)
    edges = pl.pallas_call(
        edges_kernel,
        out_shape=(edge, edge, row_edge, row_edge),
        in_specs=[hbm],
        out_specs=(vmem,) * 4,
        scratch_shapes=[
            pltpu.VMEM((2, depth, TILE, width), jnp.bfloat16),
            pltpu.VMEM((2, depth, width), jnp.float32),
            pltpu.SemaphoreType.DMA((4,)),
        ],
        compiler_params=pltpu.CompilerParams(vmem_limit_bytes=52 * MB),
        name="edges",
    )(field)

    inner_field, *edges = lax.optimization_barrier((field, *edges))

    def exchange(one, two, axis, count):
        near = [(k, k ^ 1) for k in range(count)]
        far = [(k, (k - 1 + 2 * (k & 1)) % count) for k in range(count)]
        return lax.ppermute(one, axis, near), lax.ppermute(two, axis, far)

    plane_one, plane_two = exchange(edges[0], edges[1], "depth", depth_count)
    row_one, row_two = exchange(edges[2], edges[3], "rows", row_count)

    params = (tf_centers, tf_widths, tf_density, tf_colors, light)
    cells = pltpu.VMEM((lanes + 2, depth + 2, rows + 16, LANES), jnp.float32)
    param_scratch = [pltpu.SMEM(param.shape, jnp.float32) for param in params] + [pltpu.SemaphoreType.DMA((5,))]
    scratch = [cells] + param_scratch
    compiler_params = pltpu.CompilerParams(vmem_limit_bytes=32 * MB)
    early = pl.pallas_call(
        lambda *refs: early_kernel(step_size, *refs),
        out_shape=jax.ShapeDtypeStruct((lanes, 4, rows // 2 - 8, LANES), jnp.float32),
        in_specs=[hbm] * 5 + [vmem],
        out_specs=vmem,
        scratch_shapes=scratch,
        compiler_params=compiler_params,
        cost_estimate=pl.CostEstimate(flops=30_000_000, bytes_accessed=3_000_000, transcendentals=3_000_000),
        name="early",
    )(*params, inner_field)
    halos = (plane_one, plane_two, row_one, row_two)
    half = (lanes, 4, rows // 2, LANES)
    sent = pl.pallas_call(
        lambda *refs: send_kernel(step_size, depth_count, row_count, *refs),
        out_shape=jax.ShapeDtypeStruct(half, jnp.bfloat16),
        in_specs=[hbm] * 5 + [vmem] * 6,
        out_specs=vmem,
        scratch_shapes=scratch,
        compiler_params=compiler_params,
        name="send",
    )(*params, field, *halos, early)
    keep_field, sent = lax.optimization_barrier((field, sent))
    other = lax.ppermute(sent, "depth", [(k, k ^ 1) for k in range(depth_count)])
    own = pl.pallas_call(
        lambda *refs: keep_kernel(step_size, depth_count, row_count, *refs),
        out_shape=jax.ShapeDtypeStruct(half, jnp.float32),
        in_specs=[hbm] * 5 + [vmem] * 5,
        out_specs=vmem,
        scratch_shapes=scratch,
        compiler_params=compiler_params,
        cost_estimate=pl.CostEstimate(flops=50_000_000, bytes_accessed=3_000_000, transcendentals=4_000_000),
        name="keep",
    )(*params, keep_field, *halos)
    bricks = pl.pallas_call(
        join_kernel,
        out_shape=jax.ShapeDtypeStruct((width // BAND, rows // 2, LANES), jnp.bfloat16),
        in_specs=[vmem, vmem],
        out_specs=vmem,
        compiler_params=compiler_params,
        name="join",
    )(own, other)
    bricks = lax.all_to_all(bricks, "depth", 0, 0, tiled=True)
    image = pl.pallas_call(
        compose_kernel,
        out_shape=jax.ShapeDtypeStruct((4, width // depth_count, rows), jnp.float32),
        in_specs=[vmem],
        out_specs=vmem,
        compiler_params=pltpu.CompilerParams(vmem_limit_bytes=16 * MB),
        name="compose",
    )(bricks)
    return jnp.transpose(image, (0, 2, 1))


def solution(mesh):
    placed = (P("depth", "rows", None), P(), P(), P(), P(), P())
    return jax.shard_map(
        shards, mesh=mesh, in_specs=placed, out_specs=P(None, "rows", "depth"), check_vma=False
    )
```

```python
import math

import jax
import jax.numpy as jnp
from jax import lax
from jax.experimental import pallas as pl
from jax.experimental.pallas import tpu as pltpu
from jax.sharding import PartitionSpec as P

LOG2E = math.log2(math.e)
TILE = 16
LANES = 128
BAND = 32
MB = 1024 * 1024


def dither(brick, shape):
    lane = lax.broadcasted_iota(jnp.int32, shape, 1)
    row = lax.broadcasted_iota(jnp.int32, shape, 0)
    phase = (lane * 29 + row * 13 + brick * 37) & 63
    return phase.astype(jnp.float32) * (1.0 / 64.0) + 1.0


def edges_kernel(field, plane_one, plane_two, row_one, row_two, tiles, gathered, sems):
    depth, rows, _ = field.shape
    chosen = jnp.where((lax.axis_index("depth") & 1) == 0, depth - 1, 0)
    copies = [
        pltpu.make_async_copy(field.at[:, 0:TILE], tiles.at[0], sems.at[0]),
        pltpu.make_async_copy(field.at[:, rows - TILE : rows], tiles.at[1], sems.at[1]),
        pltpu.make_async_copy(field.at[chosen], plane_one, sems.at[2]),
        pltpu.make_async_copy(field.at[depth - 1 - chosen], plane_two, sems.at[3]),
    ]
    for copy in copies:
        copy.start()
    for side, row in ((0, 0), (1, TILE - 1)):
        copies[side].wait()
        for plane in range(depth):
            tile = tiles[side, plane].astype(jnp.float32)
            gathered[side, plane : plane + 1, :] = tile[row : row + 1, :]
    even = (lax.axis_index("rows") & 1) == 0
    row_one[...] = jnp.where(even, gathered[1], gathered[0]).astype(jnp.bfloat16)
    row_two[...] = jnp.where(even, gathered[0], gathered[1]).astype(jnp.bfloat16)
    copies[2].wait()
    copies[3].wait()


def start_params(sources, targets, sems):
    copies = [
        pltpu.make_async_copy(source, target, sems.at[i]) for i, (source, target) in enumerate(zip(sources, targets))
    ]
    for copy in copies:
        copy.start()
    return copies


def shader(step_size, cells, centers, widths, density, colors, light):
    def full(scalar):
        return jnp.full((8, LANES), scalar, jnp.float32)

    count = centers.shape[0]
    center = [full(centers[k]) for k in range(count)]
    sharp = [-LOG2E / (full(widths[k]) * full(widths[k])) for k in range(count)]
    dense = [full(density[k]) * (-4.0 * LOG2E * step_size) for k in range(count)]
    lights = [full(light[k]) for k in range(3)]
    length = lax.rsqrt(lights[0] * lights[0] + lights[1] * lights[1] + lights[2] * lights[2])
    lights = [component * length * 0.7 for component in lights]
    lane = lax.broadcasted_iota(jnp.int32, (8, LANES), 1)
    at_first, at_last = lane == 0, lane == LANES - 1

    def rows_at(start):
        return pl.ds(pl.multiple_of(start + 8, 8), 8)

    def enter(j, start, plane, total=None, sums=None):
        zero = jnp.zeros((8, LANES), jnp.float32)
        before, at = cells[j + 1, plane, rows_at(start), :], cells[j + 1, plane + 1, rows_at(start), :]
        if total is None:
            return [before, at, zero, jnp.ones((8, LANES), jnp.float32)] + [zero] * count
        return [before, at, total, jnp.exp2(total)] + sums

    def step(j, start, plane, state):
        previous, current, total, clear, *sums = state
        here = rows_at(start)
        following = cells[j + 1, plane + 2, here, :]
        dz = following - previous
        dy = cells[j + 1, plane + 1, pl.ds(start + 9, 8), :] - cells[j + 1, plane + 1, pl.ds(start + 7, 8), :]
        dx = pltpu.roll(
            jnp.where(at_first, cells[j + 2, plane + 1, here, :], current), LANES - 1, 1
        ) - pltpu.roll(jnp.where(at_last, cells[j, plane + 1, here, :], current), 1, 1)
        root = lax.rsqrt(dz * dz + dy * dy + dx * dx + 4.0)
        lighting = 0.3 + jnp.abs(dz * lights[0] + dy * lights[1] + dx * lights[2]) * root
        bumps = []
        for k in range(count):
            offset = current - center[k]
            bumps.append(jnp.exp2(offset * offset * sharp[k]))
        sigma = dense[0] * bumps[0]
        weight = bumps[0] + 0.1
        for k in range(1, count):
            sigma = sigma + dense[k] * bumps[k]
            weight = weight + bumps[k]
        total = total + sigma * (0.3125 - root * root)
        remaining = jnp.exp2(total)
        factor = (clear - remaining) * lighting * pl.reciprocal(weight)
        sums = [s + factor * b for s, b in zip(sums, bumps)]
        return [current, following, total, remaining] + sums

    def mix(sums):
        mixed = []
        for c in range(3):
            colour = colors[c, 0] * sums[0]
            for k in range(1, count):
                colour = colour + colors[c, k] * sums[k]
            mixed.append(colour)
        return mixed

    return enter, step, mix


def spread(cells, plane, first, tile):
    for j in range(tile.shape[1] // LANES):
        cells[j + 1, plane, pl.ds(pl.multiple_of(8 + first, 8), TILE), :] = tile[:, LANES * j : LANES * (j + 1)]


def is_even(axis):
    return (lax.axis_index(axis) & 1) == 0


def strips_of(upper_half, rows):
    outer = jnp.where(upper_half, 0, rows - 8)
    inner = jnp.where(upper_half, 8, rows // 2)
    return [outer] + [inner + 8 * i for i in range(rows // 16 - 1)]


def tiles_of(upper_half, rows):
    base = jnp.where(upper_half, 0, rows // 2 - TILE)
    return [base + TILE * i for i in range(rows // 2 // TILE + 1)]


def zero_sides(cells, upper_half, depth, rows, lanes):
    half = pl.ds(pl.multiple_of(8 + jnp.where(upper_half, 0, rows // 2), 8), rows // 2)
    for side in (0, lanes + 1):
        for plane in range(depth):
            cells[side, plane + 1, half, :] = jnp.zeros((rows // 2, LANES), jnp.float32)


def load_tile(field, cells, plane, first):
    part = field[plane, pl.ds(pl.multiple_of(first, TILE), TILE), :]
    spread(cells, plane + 1, first, part.astype(jnp.float32))


def load_halos(
    cells, plane_one, plane_two, row_one, row_two, upper_half, depth_count, row_count, depth, rows, lanes
):
    def sided(axis, count):
        index = lax.axis_index(axis)
        return is_even(axis), (index > 0).astype(jnp.float32), (index < count - 1).astype(jnp.float32)

    def around(one, two, even, keep_lo, keep_hi):
        one, two = one.astype(jnp.float32), two.astype(jnp.float32)
        return jnp.where(even, two, one) * keep_lo, jnp.where(even, one, two) * keep_hi

    plane_sides, row_sides = sided("depth", depth_count), sided("rows", row_count)
    for first in tiles_of(upper_half, rows):
        part = pl.ds(pl.multiple_of(first, TILE), TILE)
        low, high = around(plane_one[part, :], plane_two[part, :], *plane_sides)
        spread(cells, 0, first, low)
        spread(cells, depth + 1, first, high)
    low, high = around(row_one[...], row_two[...], *row_sides)
    beside, line = jnp.where(upper_half, low, high), pl.ds(jnp.where(upper_half, 7, 8 + rows), 1)
    for j in range(lanes):
        for plane in range(depth):
            cells[j + 1, plane + 1, line, :] = beside[plane : plane + 1, LANES * j : LANES * (j + 1)]


def encode(value, scale):
    value = value * scale
    value = value * value
    value = value * value
    return (value * value).astype(jnp.bfloat16)


def decode(coded, unscale):
    return jnp.exp2(jnp.log(coded.astype(jnp.float32)) * (0.125 * LOG2E)) * unscale


def early_kernel(step_size, *refs):
    param_sources, field, out, cells, params, sems = refs[:5], refs[5], refs[6], refs[7], refs[8:13], refs[13]
    depth, rows, width = field.shape
    lanes = width // LANES
    smalls = start_params(param_sources, params, sems)
    send_upper = jnp.logical_not(is_even("depth"))
    zero_sides(cells, send_upper, depth, rows, lanes)
    firsts = tiles_of(send_upper, rows)

    def prepare(plane, carry):
        for first in firsts:
            load_tile(field, cells, plane, first)
        return carry

    lax.fori_loop(0, depth, prepare, 0)
    for copy in smalls:
        copy.wait()
    enter, step, mix = shader(step_size, cells, *params)
    starts = strips_of(send_upper, rows)[1:]

    def march(j, carry):
        states = [enter(j, start, 1) for start in starts]
        for plane in range(1, depth - 1):
            states = [step(j, start, plane, state) for start, state in zip(starts, states)]
        for i, state in enumerate(states):
            for c, value in enumerate(mix(state[4:]) + [state[2]]):
                out[j, c, 8 * i : 8 * i + 8, :] = value
        return carry

    lax.fori_loop(0, lanes, march, 0)


def send_kernel(step_size, depth_count, row_count, *refs):
    param_sources, field, plane_one, plane_two, row_one, row_two, early, out = refs[:5], *refs[5:12]
    cells, params, sems = refs[12], refs[13:18], refs[18]
    depth, rows, width = field.shape
    lanes = width // LANES
    smalls = start_params(param_sources, params, sems)
    send_upper = jnp.logical_not(is_even("depth"))
    zero_sides(cells, send_upper, depth, rows, lanes)
    firsts = tiles_of(send_upper, rows)
    load_halos(cells, plane_one, plane_two, row_one, row_two, send_upper, depth_count, row_count, depth, rows, lanes)
    outer = jnp.where(send_upper, 0, rows - TILE)

    def prepare(plane, carry):
        load_tile(field, cells, plane, outer)
        return carry

    lax.fori_loop(0, depth, prepare, 0)
    for plane in (0, 1, depth - 2, depth - 1):
        for first in firsts:
            load_tile(field, cells, plane, first)
    for copy in smalls:
        copy.wait()
    enter, step, mix = shader(step_size, cells, *params)
    starts = strips_of(send_upper, rows)
    scale = dither(lax.axis_index("depth"), (TILE, LANES)) * 65536.0

    def march(j, carry):
        state = enter(j, starts[0], 0)
        for plane in range(depth):
            state = step(j, starts[0], plane, state)
        strips = [mix(state[4:]) + [-state[2]]]
        for i, start in enumerate(starts[1:]):
            state = step(j, start, 0, enter(j, start, 0))
            front, total = state[3], state[2] + early[j, 3, 8 * i : 8 * i + 8, :]
            state = step(j, start, depth - 1, enter(j, start, depth - 1, total, state[4:]))
            values = [v + front * early[j, c, 8 * i : 8 * i + 8, :] for c, v in enumerate(mix(state[4:]))]
            strips.append(values + [-state[2]])
        for c in range(4):
            for i in range(0, len(strips), 2):
                both = jnp.concatenate([strips[i][c], strips[i + 1][c]], axis=0)
                out[j, c, 8 * i : 8 * i + 16, :] = encode(both, scale)
        return carry

    lax.fori_loop(0, lanes, march, 0)


def keep_kernel(step_size, depth_count, row_count, *refs):
    param_sources, field, plane_one, plane_two, row_one, row_two, out = refs[:5], *refs[5:11]
    cells, params, sems = refs[11], refs[12:17], refs[17]
    depth, rows, width = field.shape
    lanes = width // LANES
    smalls = start_params(param_sources, params, sems)
    keep_upper = is_even("depth")
    zero_sides(cells, keep_upper, depth, rows, lanes)
    firsts = tiles_of(keep_upper, rows)
    load_halos(cells, plane_one, plane_two, row_one, row_two, keep_upper, depth_count, row_count, depth, rows, lanes)

    def prepare(plane, carry):
        for first in firsts:
            load_tile(field, cells, plane, first)
        return carry

    lax.fori_loop(0, depth, prepare, 0)
    for copy in smalls:
        copy.wait()
    enter, step, mix = shader(step_size, cells, *params)
    starts = strips_of(keep_upper, rows)

    def march(j, carry):
        done = []
        for i in range(0, len(starts), 4):
            pair = starts[i : i + 4]
            states = [enter(j, start, 0) for start in pair]
            for plane in range(depth):
                states = [step(j, start, plane, state) for start, state in zip(pair, states)]
            done += [mix(state[4:]) + [-state[2]] for state in states]
        for i, values in enumerate(done):
            for c in range(4):
                out[j, c, 8 * i : 8 * i + 8, :] = values[c]
        return carry

    lax.fori_loop(0, lanes, march, 0)


def join_kernel(own, other, out):
    lanes = own.shape[0]
    me, even = lax.axis_index("depth"), is_even("depth")
    unscale = 1.0 / (dither(me + 1 - 2 * (me & 1), (TILE, LANES)) * 65536.0)
    scale = dither(me, (TILE, LANES)) * 32768.0
    lane = lax.broadcasted_iota(jnp.int32, (8, LANES), 1)
    upper, odd = lane >= 64, (lane & BAND) > 0

    def exchange(a, b, mask, shift):
        moved = pltpu.roll(jnp.where(mask, a, b), shift, 1)
        return jnp.where(mask, moved, a), jnp.where(mask, b, moved)

    def one(j):
        bands = [[], [], [], []]
        joined = [[] for _ in range(4)]
        for half in range(2):
            part = slice(TILE * half, TILE * (half + 1))
            mine = [own[j, c, part, :] for c in range(4)]
            theirs = [decode(other[j, c, part, :], unscale) for c in range(4)]
            front = jnp.exp2(-jnp.where(even, mine[3], theirs[3]))
            for c in range(3):
                first, second = jnp.where(even, mine[c], theirs[c]), jnp.where(even, theirs[c], mine[c])
                joined[c].append(first + front * second)
            joined[3].append(mine[3] + theirs[3])
        for c in range(4):
            strip = [joined[c][i // 2][8 * (i % 2) : 8 * (i % 2) + 8, :] for i in range(4)]
            strip[0], strip[2] = exchange(strip[0], strip[2], upper, 64)
            strip[1], strip[3] = exchange(strip[1], strip[3], upper, 64)
            strip[0], strip[1] = exchange(strip[0], strip[1], odd, BAND)
            strip[2], strip[3] = exchange(strip[2], strip[3], odd, BAND)
            for band in range(4):
                bands[band].append(strip[band])
        for band in range(4):
            for c in (0, 2):
                both = jnp.concatenate([bands[band][c], bands[band][c + 1]], axis=0)
                out[4 * j + band, 8 * c : 8 * c + 16, :] = encode(both, scale)

    for j in range(lanes):
        one(j)


def compose_kernel(bricks, out):
    count = bricks.shape[0]
    halves = []
    for half in range(2):
        total = jnp.zeros((8, LANES), jnp.float32)
        image = [jnp.zeros((8, LANES), jnp.float32) for _ in range(3)]
        for brick in range(half, count, 2):
            unscale = 1.0 / (dither(brick, (TILE, LANES)) * 32768.0)
            values = []
            for c in (0, 2):
                both = decode(bricks[brick, 8 * c : 8 * c + 16, :], unscale)
                values += [both[:8], both[8:]]
            front = jnp.exp2(-total)
            image = [sofar + front * value for sofar, value in zip(image, values)]
            total = total + values[3]
        halves.append(image + [1.0 - jnp.exp2(-total)])
    odd = jnp.logical_not(is_even("depth"))
    for c in range(4):
        turned = jnp.concatenate([halves[0][c], halves[1][c]], axis=0).T
        block = [turned[BAND * q : BAND * (q + 1), :] for q in range(4)]
        block[0], block[2] = jnp.where(odd, block[2], block[0]), jnp.where(odd, block[0], block[2])
        out[c] = jnp.concatenate(
            [block[q][:, :8] for q in (0, 1, 2, 3)] + [block[q][:, 8:] for q in (1, 2, 3, 0)], axis=1
        )


def shards(field, tf_centers, tf_widths, tf_density, tf_colors, light):
    depth_count, row_count = lax.axis_size("depth"), lax.axis_size("rows")
    depth, rows, width = field.shape
    lanes = width // LANES
    step_size = 0.5 / (depth * depth_count)
    hbm, vmem = pl.BlockSpec(memory_space=pltpu.HBM), pl.BlockSpec(memory_space=pltpu.VMEM)

    edge = jax.ShapeDtypeStruct((rows, width), jnp.bfloat16)
    row_edge = jax.ShapeDtypeStruct((depth, width), jnp.bfloat16)
    edges = pl.pallas_call(
        edges_kernel,
        out_shape=(edge, edge, row_edge, row_edge),
        in_specs=[hbm],
        out_specs=(vmem,) * 4,
        scratch_shapes=[
            pltpu.VMEM((2, depth, TILE, width), jnp.bfloat16),
            pltpu.VMEM((2, depth, width), jnp.float32),
            pltpu.SemaphoreType.DMA((4,)),
        ],
        compiler_params=pltpu.CompilerParams(vmem_limit_bytes=52 * MB),
        name="edges",
    )(field)

    inner_field, *edges = lax.optimization_barrier((field, *edges))

    def exchange(one, two, axis, count):
        near = [(k, k ^ 1) for k in range(count)]
        far = [(k, (k - 1 + 2 * (k & 1)) % count) for k in range(count)]
        return lax.ppermute(one, axis, near), lax.ppermute(two, axis, far)

    plane_one, plane_two = exchange(edges[0], edges[1], "depth", depth_count)
    row_one, row_two = exchange(edges[2], edges[3], "rows", row_count)

    params = (tf_centers, tf_widths, tf_density, tf_colors, light)
    cells = pltpu.VMEM((lanes + 2, depth + 2, rows + 16, LANES), jnp.float32)
    param_scratch = [pltpu.SMEM(param.shape, jnp.float32) for param in params] + [pltpu.SemaphoreType.DMA((5,))]
    scratch = [cells] + param_scratch
    compiler_params = pltpu.CompilerParams(vmem_limit_bytes=32 * MB)
    early = pl.pallas_call(
        lambda *refs: early_kernel(step_size, *refs),
        out_shape=jax.ShapeDtypeStruct((lanes, 4, rows // 2 - 8, LANES), jnp.float32),
        in_specs=[hbm] * 5 + [vmem],
        out_specs=vmem,
        scratch_shapes=scratch,
        compiler_params=compiler_params,
        cost_estimate=pl.CostEstimate(flops=30_000_000, bytes_accessed=3_000_000, transcendentals=3_000_000),
        name="early",
    )(*params, inner_field)
    halos = (plane_one, plane_two, row_one, row_two)
    half = (lanes, 4, rows // 2, LANES)
    sent = pl.pallas_call(
        lambda *refs: send_kernel(step_size, depth_count, row_count, *refs),
        out_shape=jax.ShapeDtypeStruct(half, jnp.bfloat16),
        in_specs=[hbm] * 5 + [vmem] * 6,
        out_specs=vmem,
        scratch_shapes=scratch,
        compiler_params=compiler_params,
        name="send",
    )(*params, field, *halos, early)
    keep_field, sent = lax.optimization_barrier((field, sent))
    other = lax.ppermute(sent, "depth", [(k, k ^ 1) for k in range(depth_count)])
    own = pl.pallas_call(
        lambda *refs: keep_kernel(step_size, depth_count, row_count, *refs),
        out_shape=jax.ShapeDtypeStruct(half, jnp.float32),
        in_specs=[hbm] * 5 + [vmem] * 5,
        out_specs=vmem,
        scratch_shapes=scratch,
        compiler_params=compiler_params,
        cost_estimate=pl.CostEstimate(flops=50_000_000, bytes_accessed=3_000_000, transcendentals=4_000_000),
        name="keep",
    )(*params, keep_field, *halos)
    bricks = pl.pallas_call(
        join_kernel,
        out_shape=jax.ShapeDtypeStruct((width // BAND, rows // 2, LANES), jnp.bfloat16),
        in_specs=[vmem, vmem],
        out_specs=vmem,
        compiler_params=compiler_params,
        name="join",
    )(own, other)
    bricks = lax.all_to_all(bricks, "depth", 0, 0, tiled=True)
    image = pl.pallas_call(
        compose_kernel,
        out_shape=jax.ShapeDtypeStruct((4, width // depth_count, rows), jnp.float32),
        in_specs=[vmem],
        out_specs=vmem,
        compiler_params=pltpu.CompilerParams(vmem_limit_bytes=16 * MB),
        name="compose",
    )(bricks)
    return jnp.transpose(image, (0, 2, 1))


def solution(mesh):
    placed = (P("depth", "rows", None), P(), P(), P(), P(), P())
    return jax.shard_map(
        shards, mesh=mesh, in_specs=placed, out_specs=P(None, "rows", "depth"), check_vma=False
    )
```
